32 devices in a mesh: grp: 1, row: 8 (over z, core), col: 4 (over y, x).
Axes of the slice: x: 2, y: 2, z: 4, core: 2. Of those that a mesh axis runs over, the one named last changes fastest.
Arguments:
- ocean_field: bfloat16 [64, 128, 128, 128], P('grp', 'row', 'col'), may hold values from -6 to 6
- spec_first: bfloat16 [2, 32, 64, 64], replicated, may hold values from -0.5 to 0.5
- spec_second: bfloat16 [2, 32, 64, 64], replicated, may hold values from -0.5 to 0.5
- spec_third: bfloat16 [2, 32, 64, 64], replicated, may hold values from -0.5 to 0.5
- ffn_in: bfloat16 [64, 256], replicated, may hold values from -0.75 to 0.75
- ffn_out: bfloat16 [256, 64], replicated, may hold values from -0.375 to 0.375
- bias_in: float32 [256], replicated, may hold values from -3 to 3
- bias_out: float32 [64], replicated, may hold values from -3 to 3
Outputs:
- next_field: bfloat16 [64, 128, 128, 128], P('grp', 'row', 'col')
The draws below stay inside these ranges and needn't reach their ends.
All inputs are finite; a program needn't handle non-finite values.
Results may differ from the reference program's by a relative error of at most 0.013.
Values may be sent and summed in bfloat16 or wider, within the bound.
No kernel may reach another device: no remote copies, remote signals or barrier semaphores. Data moves between devices by JAX's collectives and lax.ppermute only.
A program may use at most 192 MiB of HBM per device.

```python
import math
import jax
import jax.numpy as jnp
from jax import lax

C = 64
H = 256
M = 32
N1 = 128
N2 = 128
N3 = 128


def shard_levels(rng, dims, split, least, largest):
    loudness = 1.0
    for axis_at, shards_of in split:
        steps = jax.random.uniform(jax.random.fold_in(jax.random.fold_in(rng, 6), axis_at), (shards_of,), jnp.float32, least / len(split), largest / len(split))
        loudness = loudness * jnp.repeat(jnp.exp(steps), dims[axis_at] // shards_of).reshape((-1,) + (1,) * (len(dims) - 1 - axis_at))
    return loudness


def scatter_about(key, dims, deviation, most, split=(), kind=jnp.bfloat16):
    entries = jax.random.normal(key, dims, jnp.float32) * deviation
    if len(split) > 0:
        entries = shard_levels(key, dims, split, -0.22, 0.18) * entries
    return jnp.clip(entries, min=-most, max=most).astype(kind)


def setup_inputs(seed: int = 0, part: int = 0) -> dict:
    arg_keys = jax.random.split(jax.random.key(seed), 9)
    part_splits = jax.random.split(jax.random.fold_in(arg_keys[8], part), 9)
    ocean_field = scatter_about(part_splits[0], (C, N1, N2, N3), 1.0, 6.0, ((1, 8), (2, 4)))
    spec_first = scatter_about(arg_keys[1], (2, M, C, C), (2 * C) ** -0.5, 0.5)
    spec_second = scatter_about(arg_keys[2], (2, M, C, C), (2 * C) ** -0.5, 0.5)
    spec_third = scatter_about(arg_keys[3], (2, M, C, C), (2 * C) ** -0.5, 0.5)
    ffn_in = scatter_about(arg_keys[4], (C, H), C ** -0.5, 0.75)
    ffn_out = scatter_about(arg_keys[5], (H, C), H ** -0.5, 0.375)
    bias_in = scatter_about(arg_keys[6], (H,), 0.5, 3.0, (), jnp.float32)
    bias_out = scatter_about(arg_keys[7], (C,), 0.5, 3.0, (), jnp.float32)
    return dict(ocean_field=ocean_field, spec_first=spec_first, spec_second=spec_second, spec_third=spec_third, ffn_in=ffn_in, ffn_out=ffn_out, bias_in=bias_in, bias_out=bias_out)


def forward_table(length, mode_count):
    grid_pos = jnp.arange(length, dtype=jnp.int32)[:, None]
    mode_location = jnp.arange(mode_count, dtype=jnp.int32)[None, :]
    phase = ((grid_pos * mode_location) % length).astype(jnp.float32) * (2.0 * math.pi / length)
    return jnp.stack([jnp.cos(phase), -jnp.sin(phase)], axis=1).astype(jnp.bfloat16)


def inverse_table(length, mode_count):
    mode_location = jnp.arange(mode_count, dtype=jnp.int32)[:, None]
    grid_pos = jnp.arange(length, dtype=jnp.int32)[None, :]
    phase = ((grid_pos * mode_location) % length).astype(jnp.float32) * (2.0 * math.pi / length)
    factor = jnp.where(mode_location == 0, 1.0, 2.0).astype(jnp.float32) / length
    return jnp.stack([factor * jnp.cos(phase), -factor * jnp.sin(phase)], axis=0).astype(jnp.bfloat16)


def block_weight_tensor(weight_tensor):
    real_part = weight_tensor[0]
    imag_part = weight_tensor[1]
    upper = jnp.concatenate([real_part, imag_part], axis=2)
    lower = jnp.concatenate([-imag_part, real_part], axis=2)
    return jnp.concatenate([upper, lower], axis=1)


def precise_contraction(form, left, right):
    return jnp.einsum(form, left.astype(jnp.float32), right.astype(jnp.float32), precision=lax.Precision.HIGHEST)


def along_axis(values, weight_tensor):
    channels, across, length, columns = values.shape
    mode_count = weight_tensor.shape[1]
    spectral_coefficients = precise_contraction("canq,nsm->mscaq", values, forward_table(length, mode_count))
    spectral_coefficients = spectral_coefficients.reshape(mode_count, 2 * channels, across * columns).astype(jnp.bfloat16)
    mixed_result = precise_contraction("plf,plk->pkf", spectral_coefficients, block_weight_tensor(weight_tensor))
    mixed_result = mixed_result.astype(jnp.bfloat16).reshape(mode_count, 2, channels, across, columns)
    result = precise_contraction("mscaq,smn->canq", mixed_result, inverse_table(length, mode_count))
    return result.astype(jnp.bfloat16)


def final_axis_transform(values, weight_tensor):
    channels, places, length = values.shape
    mode_count = weight_tensor.shape[1]
    spectral_coefficients = precise_contraction("cpn,nsm->mscp", values, forward_table(length, mode_count))
    spectral_coefficients = spectral_coefficients.reshape(mode_count, 2 * channels, places).astype(jnp.bfloat16)
    mixed_result = precise_contraction("plf,plk->pkf", spectral_coefficients, block_weight_tensor(weight_tensor))
    mixed_result = mixed_result.astype(jnp.bfloat16).reshape(mode_count, 2, channels, places)
    result = precise_contraction("mscp,smn->cpn", mixed_result, inverse_table(length, mode_count))
    return result.astype(jnp.bfloat16)


def feed_forward(summed, initial, ffn_in, ffn_out, bias_in, bias_out):
    def update(position, output):
        row_index = jnp.asarray(position).astype(jnp.int32)
        block = lax.dynamic_index_in_dim(summed, row_index, 1, keepdims=False)
        base = lax.dynamic_index_in_dim(initial, row_index, 1, keepdims=False)
        hidden_pre = precise_contraction("ch,ck->hk", ffn_in, block) + bias_in[:, None]
        hidden = jax.nn.gelu(hidden_pre, approximate=False).astype(jnp.bfloat16)
        result = precise_contraction("hc,hk->ck", ffn_out, hidden) + bias_out[:, None] + base.astype(jnp.float32)
        return lax.dynamic_update_index_in_dim(output, result.astype(jnp.bfloat16), row_index, 1)
    return lax.fori_loop(0, summed.shape[1], update, jnp.zeros_like(initial))


def reference(ocean_field, spec_first, spec_second, spec_third, ffn_in, ffn_out, bias_in, bias_out):
    first_part = along_axis(ocean_field.reshape(C, 1, N1, N2 * N3), spec_first).reshape(C, N1, N2, N3)
    second_part = along_axis(ocean_field, spec_second)
    third_part = final_axis_transform(ocean_field.reshape(C, N1 * N2, N3), spec_third).reshape(C, N1, N2, N3)
    pair = (first_part.astype(jnp.float32) + second_part.astype(jnp.float32)).astype(jnp.bfloat16)
    summed = (pair.astype(jnp.float32) + third_part.astype(jnp.float32)).astype(jnp.bfloat16)
    result = feed_forward(summed.reshape(C, N1, N2 * N3), ocean_field.reshape(C, N1, N2 * N3), ffn_in, ffn_out, bias_in, bias_out)
    return result.reshape(C, N1, N2, N3)
```

```python
import functools
import math

import jax
import jax.numpy as jnp
from jax import lax
from jax.experimental import pallas as pl
from jax.experimental.pallas import tpu as pltpu
from jax.sharding import PartitionSpec as P

MIB = 1024 * 1024
HALF_ROOT = math.sqrt(0.5)


def forward_rows(length, mode_count):
    grid_pos = jnp.arange(length, dtype=jnp.int32)[None, :]
    mode_location = jnp.arange(mode_count, dtype=jnp.int32)[:, None]
    phase = (grid_pos * mode_location % length).astype(jnp.float32) * (2.0 * math.pi / length)
    return jnp.concatenate([jnp.cos(phase), -jnp.sin(phase)], axis=0).astype(jnp.bfloat16)


def inverse_rows(length, mode_count):
    mode_location = jnp.arange(mode_count, dtype=jnp.int32)[:, None]
    grid_pos = jnp.arange(length, dtype=jnp.int32)[None, :]
    phase = (grid_pos * mode_location % length).astype(jnp.float32) * (2.0 * math.pi / length)
    factor = jnp.where(mode_location == 0, 1.0, 2.0).astype(jnp.float32) / length
    return jnp.concatenate(
        [factor * jnp.cos(phase), -factor * jnp.sin(phase)], axis=0
    ).astype(jnp.bfloat16)


def mix_kernel(*refs):
    count = len(refs) // 2
    for spec, out in zip(refs[:count], refs[count:]):
        channels = spec.shape[-1]
        for mode in range(spec.shape[1]):
            real = spec[0, mode].astype(jnp.float32).T
            imag = spec[1, mode].astype(jnp.float32).T
            upper = jnp.concatenate([real, -imag], axis=1)
            lower = jnp.concatenate([imag, real], axis=1)
            out[mode, :channels] = upper.astype(jnp.bfloat16)
            out[mode, channels:] = lower.astype(jnp.bfloat16)


def mix_rows(after, *specs):
    _, mode_count, channels, _ = specs[0].shape
    block = min(8, mode_count)
    kernel, token_specs, token = ordered(mix_kernel, after)
    return pl.pallas_call(
        kernel,
        grid=(mode_count // block,),
        in_specs=token_specs
        + [pl.BlockSpec((2, block, channels, channels), lambda g: (0, g, 0, 0))]
        * len(specs),
        out_specs=[pl.BlockSpec((block, 2 * channels, 2 * channels), lambda g: (g, 0, 0))]
        * len(specs),
        out_shape=[
            jax.ShapeDtypeStruct((mode_count, 2 * channels, 2 * channels), jnp.bfloat16)
        ]
        * len(specs),
        compiler_params=pltpu.CompilerParams(vmem_limit_bytes=12 * MIB),
        cost_estimate=cost(2.5, 4 * MIB),
        name="mixing_matrices",
    )(*token, *specs)


def cost(micros, size):
    return pl.CostEstimate(
        flops=int(micros * 1.15e9), bytes_accessed=int(size), transcendentals=0
    )


def ordered(kernel, after):
    if after is None:
        return kernel, [], []
    return (
        lambda _, *refs: kernel(*refs),
        [pl.BlockSpec(memory_space=pl.ANY)],
        [after],
    )


def mm(left, right, dims=(1, 0)):
    return lax.dot_general(
        left, right, (((dims[0],), (dims[1],)), ((), ())), preferred_element_type=jnp.float32
    )


def stack_rows(parts):
    if parts[0].shape[0] % 16 == 0:
        return jnp.concatenate(parts, axis=0)
    return jnp.concatenate([p.astype(jnp.float32) for p in parts], axis=0).astype(jnp.bfloat16)


def partners(ways):
    steps, half = [0], ways // 2
    while half:
        steps += range(half, 2 * half)
        half //= 2
    return steps


def pack_kernel(ways, me_ref, x_ref, *refs):
    outs, wide = refs[:ways], refs[ways]
    channels, rows, _, lanes = x_ref.shape
    wide[...] = x_ref[...].astype(jnp.float32).reshape(channels * rows * ways, lanes)
    for out, step in zip(outs, partners(ways)):
        picked = wide[pl.ds(me_ref[0] ^ step, channels * rows, stride=ways), :]
        out[...] = picked.reshape(channels, rows, lanes).astype(jnp.bfloat16)


def pack(field, first, count, ways, me, after):
    channels, rows, _, lanes = field.shape
    depth = min(16, channels)
    token_specs = [] if after is None else [pl.BlockSpec(memory_space=pl.ANY)]
    token = [] if after is None else [after]

    def kernel(me_ref, x_ref, *refs):
        pack_kernel(ways, me_ref, x_ref, *refs[len(token) :])

    return pl.pallas_call(
        kernel,
        grid_spec=pltpu.PrefetchScalarGridSpec(
            num_scalar_prefetch=1,
            grid=(count, channels // depth),
            in_specs=[
                pl.BlockSpec((depth, rows, ways, lanes), lambda k, g, me: (g, 0, first + k, 0))
            ]
            + token_specs,
            out_specs=[pl.BlockSpec((None, depth, rows, lanes), lambda k, g, me: (k, g, 0, 0))]
            * ways,
            scratch_shapes=[pltpu.VMEM((depth * rows * ways, lanes), jnp.float32)],
        ),
        out_shape=[jax.ShapeDtypeStruct((count, channels, rows, lanes), jnp.bfloat16)] * ways,
        compiler_params=pltpu.CompilerParams(vmem_limit_bytes=12 * MIB),
        cost_estimate=cost(3 * count, 4 * count * channels * rows * ways * lanes),
        name="pack_columns",
    )(me, field, *token)


def side_kernel(x_ref, _, out_ref):
    out_ref[...] = x_ref[...]


def rows_first(field, after):
    channels, rows, cols, lanes = field.shape
    return pl.pallas_call(
        side_kernel,
        grid=(rows,),
        in_specs=[
            pl.BlockSpec((channels, None, cols, lanes), lambda r: (0, r, 0, 0)),
            pl.BlockSpec(memory_space=pl.ANY),
        ],
        out_specs=pl.BlockSpec((None, channels, cols, lanes), lambda r: (r, 0, 0, 0)),
        out_shape=jax.ShapeDtypeStruct((rows, channels, cols, lanes), jnp.bfloat16),
        compiler_params=pltpu.CompilerParams(vmem_limit_bytes=12 * MIB),
        cost_estimate=cost(6, 16 * MIB),
        name="rows_first",
    )(field, after)


def mix_modes(mix_ref, spectra, mixed):
    mode_count, depth, _ = mix_ref.shape
    channels = depth // 2

    def one(mode, _):
        block = spectra[pl.ds(pl.multiple_of(mode * depth, depth), depth), :].astype(jnp.bfloat16)
        result = mm(mix_ref[mode], block)
        for part in range(2):
            mixed[pl.ds(part * mode_count + mode, channels, stride=2 * mode_count), :] = result[
                part * channels : (part + 1) * channels
            ]
        return 0

    lax.fori_loop(0, mode_count, one, 0, unroll=4)


def keep_spectra(spectra, result, channel, mode_count, channels, lanes):
    for at in range(2):
        for part in range(2):
            spectra[pl.ds(part * channels + channel + at, mode_count, stride=2 * channels), :] = (
                result[part * mode_count : (part + 1) * mode_count, at * lanes : (at + 1) * lanes]
            )


def mixed_pair(mixed, channel, coefs):
    start = pl.multiple_of(channel * coefs, 2 * coefs)
    return jnp.concatenate(
        [mixed[pl.ds(start, coefs), :], mixed[pl.ds(start + coefs, coefs), :]], axis=1
    ).astype(jnp.bfloat16)


def lines_kernel(ways, ft_ref, it_ref, mix_ref, *refs):
    count = (len(refs) - 3) // 2
    pieces, outs = refs[:count], refs[count : 2 * count]
    spectra, mixed, wide = refs[2 * count :]
    if count < ways:
        pieces = [pieces[0].at[step] for step in range(ways)]
        outs = [outs[0].at[step] for step in range(ways)]
    channels, length, lanes = pieces[0].shape
    mode_count = mix_ref.shape[0]
    total = ways * length

    def forward(pair, _):
        channel = 2 * pair
        right = jnp.concatenate(
            [stack_rows([piece[channel + at] for piece in pieces]) for at in range(2)], axis=1
        )
        keep_spectra(spectra, mm(ft_ref[...], right), channel, mode_count, channels, lanes)
        return 0

    lax.fori_loop(0, channels // 2, forward, 0, unroll=4)
    mix_modes(mix_ref, spectra, mixed)

    def inverse(pair, _):
        channel = 2 * pair
        result = mm(it_ref[...], mixed_pair(mixed, channel, 2 * mode_count))
        for at in range(2):
            wide[pl.ds(channel + at, total, stride=channels), :] = result[
                :, at * lanes : (at + 1) * lanes
            ]
        return 0

    lax.fori_loop(0, channels // 2, inverse, 0, unroll=4)
    for step in range(ways):
        part = wide[pl.ds(step * length * channels, length * channels), :]
        outs[step][...] = part.reshape(length, channels, lanes).astype(jnp.bfloat16)


def transform_cost(channels, mode_count, length, lines):
    macs = lines * channels * mode_count * 2 * (2 * length + 2 * channels)
    return cost(macs * 5e-8, 4 * lines * channels * length)


def along_lines(pieces, weights, order=None, which=None, after=None):
    stacked = not isinstance(pieces, list)
    if stacked:
        ways, across, channels, length, lanes = pieces.shape
        pieces = [pieces]
        piece_spec = pl.BlockSpec(
            (ways, None, channels, length, lanes), lambda g: (0, g, 0, 0, 0)
        )
        out_spec = pl.BlockSpec((ways, None, length, channels, lanes), lambda g: (0, g, 0, 0, 0))
        out_shape = (ways, across, length, channels, lanes)
    else:
        ways = len(pieces)
        begin, across = which
        _, channels, length, lanes = pieces[0].shape
        piece_spec = pl.BlockSpec(
            (None, channels, length, lanes), lambda g: (begin + g, 0, 0, 0)
        )
        out_spec = pl.BlockSpec((None, length, channels, lanes), lambda g: (g, 0, 0, 0))
        out_shape = (across, length, channels, lanes)
    mode_count = weights.shape[0]
    total = ways * length
    forward = forward_rows(total, mode_count)
    back = inverse_rows(total, mode_count).T
    if not stacked:
        forward = forward.reshape(2 * mode_count, ways, length)
        forward = jnp.take(forward, order, axis=1).reshape(2 * mode_count, total)
        back = back.reshape(ways, length, 2 * mode_count)
        back = jnp.take(back, order, axis=0).reshape(total, 2 * mode_count)
    whole = lambda shape: pl.BlockSpec(shape, lambda g: (0,) * len(shape))
    kernel, token_specs, token = ordered(functools.partial(lines_kernel, ways), after)
    return pl.pallas_call(
        kernel,
        grid=(across,),
        in_specs=token_specs
        + [whole(forward.shape), whole(back.shape), whole(weights.shape)]
        + [piece_spec] * len(pieces),
        out_specs=[out_spec] * len(pieces),
        out_shape=[jax.ShapeDtypeStruct(out_shape, jnp.bfloat16)] * len(pieces),
        scratch_shapes=[
            pltpu.VMEM((2 * channels * mode_count, lanes), jnp.float32),
            pltpu.VMEM((2 * channels * mode_count, lanes), jnp.float32),
            pltpu.VMEM((total * channels, lanes), jnp.float32),
        ],
        compiler_params=pltpu.CompilerParams(vmem_limit_bytes=26 * MIB),
        cost_estimate=transform_cost(channels, mode_count, total, across * lanes),
        name="line_branch",
    )(*token, forward, back, weights, *pieces)


def last_kernel(ft_ref, it_ref, mix_ref, x_ref, out_ref, spectra, mixed, wide):
    channels, rows, cols, length = x_ref.shape
    mode_count = mix_ref.shape[0]
    cells = rows * cols

    def forward(pair, _):
        channel = 2 * pair
        right = jnp.concatenate(
            [x_ref[channel + at].reshape(cells, length) for at in range(2)], axis=0
        )
        keep_spectra(
            spectra, mm(ft_ref[...], right, (1, 1)), channel, mode_count, channels, cells
        )
        return 0

    lax.fori_loop(0, channels // 2, forward, 0, unroll=4)
    mix_modes(mix_ref, spectra, mixed)

    def inverse(pair, _):
        channel = 2 * pair
        result = mm(mixed_pair(mixed, channel, 2 * mode_count), it_ref[...], (0, 0))
        for at in range(2):
            wide[pl.ds(channel + at, cells, stride=channels), :] = result[
                at * cells : (at + 1) * cells
            ]
        return 0

    lax.fori_loop(0, channels // 2, inverse, 0, unroll=4)
    out_ref[...] = wide[...].reshape(rows, cols, channels, length).astype(jnp.bfloat16)


def last_branch(field, weights, part, parts, done, after):
    channels, rows, cols, length = field.shape
    mode_count = weights.shape[0]
    block = max(1, min(rows // parts, 128 // cols))
    steps = rows // block // parts
    forward, back = forward_rows(length, mode_count), inverse_rows(length, mode_count)
    whole = lambda shape: pl.BlockSpec(shape, lambda g: (0,) * len(shape))
    _, token_specs, token = ordered(last_kernel, after)
    aliases = {}
    if done is not None:
        token_specs, token = token_specs + [pl.BlockSpec(memory_space=pl.ANY)], token + [done]
        aliases = {len(token) - 1: 0}
    skipped = len(token)
    return pl.pallas_call(
        lambda *refs: last_kernel(*refs[skipped:]),
        grid=(steps,),
        in_specs=token_specs
        + [
            whole(forward.shape),
            whole(back.shape),
            whole(weights.shape),
            pl.BlockSpec(
                (channels, block, cols, length), lambda g: (0, part * steps + g, 0, 0)
            ),
        ],
        out_specs=pl.BlockSpec(
            (block, cols, channels, length), lambda g: (part * steps + g, 0, 0, 0)
        ),
        out_shape=jax.ShapeDtypeStruct((rows, cols, channels, length), jnp.bfloat16),
        input_output_aliases=aliases,
        scratch_shapes=[
            pltpu.VMEM((2 * channels * mode_count, block * cols), jnp.float32),
            pltpu.VMEM((2 * channels * mode_count, block * cols), jnp.float32),
            pltpu.VMEM((block * cols * channels, length), jnp.float32),
        ],
        compiler_params=pltpu.CompilerParams(vmem_limit_bytes=26 * MIB),
        cost_estimate=transform_cost(channels, mode_count, length, steps * block * cols),
        name="last_branch",
    )(*token, forward, back, weights, field)


def cell_kernel(ways, me_ref, x_ref, win_ref, wout_ref, bin_ref, bout_ref, *refs):
    first = refs[:ways]
    second, third = refs[ways : ways + 2]
    out_ref, wide = refs[-2:]
    channels, _, _, lanes = x_ref.shape
    steps = partners(ways)
    for place in range(0, ways, 2):
        summed = []
        for at in range(2):
            col = me_ref[0] ^ steps[place + at]
            pair = first[place + at][...].astype(jnp.float32) + second[col].astype(jnp.float32)
            pair = pair.astype(jnp.bfloat16).astype(jnp.float32)
            summed.append((pair + third[col].astype(jnp.float32)).astype(jnp.bfloat16))
        pre = mm(win_ref[...], jnp.concatenate(summed, axis=1)) + bin_ref[...]
        hidden = (0.5 * pre * (1.0 + lax.erf(pre * HALF_ROOT))).astype(jnp.bfloat16)
        result = mm(wout_ref[...], hidden) + bout_ref[...]
        for at in range(2):
            col = me_ref[0] ^ steps[place + at]
            wide[pl.ds(col, channels, stride=ways), :] = result[:, at * lanes : (at + 1) * lanes]
    total = wide[...].reshape(channels, ways, lanes) + x_ref[:, 0].astype(jnp.float32)
    out_ref[:, 0] = total.astype(jnp.bfloat16)


def cells(field, first, which, second, third, ffn, chunk, me, done):
    channels, rows, cols, lanes = field.shape
    ways = len(first)
    whole = lambda shape: pl.BlockSpec(shape, lambda *_: (0,) * len(shape))
    tile = pl.BlockSpec((channels, 1, ways, lanes), lambda r, me: (0, r, chunk, 0))
    branch = pl.BlockSpec((None, ways, channels, lanes), lambda r, me: (r, chunk, 0, 0))
    in_specs = [tile] + [whole(w.shape) for w in ffn]
    in_specs += [
        pl.BlockSpec((None, None, channels, lanes), lambda r, me: (which, r, 0, 0))
    ] * ways
    in_specs += [branch, branch]
    operands = [me, field, *ffn, *first, second, third]
    aliases = {}
    if done is not None:
        in_specs.append(pl.BlockSpec(memory_space=pl.ANY))
        aliases = {len(operands): 0}
        operands.append(done)
    hidden = ffn[0].shape[0]
    count = rows * ways * lanes
    return pl.pallas_call(
        functools.partial(cell_kernel, ways),
        grid_spec=pltpu.PrefetchScalarGridSpec(
            num_scalar_prefetch=1,
            grid=(rows,),
            in_specs=in_specs,
            out_specs=tile,
            scratch_shapes=[pltpu.VMEM((channels * ways, lanes), jnp.float32)],
        ),
        out_shape=jax.ShapeDtypeStruct(field.shape, jnp.bfloat16),
        input_output_aliases=aliases,
        compiler_params=pltpu.CompilerParams(vmem_limit_bytes=16 * MIB),
        cost_estimate=cost(4.6e-6 * count * hidden, 10 * count * channels),
        name="feed_forward",
    )(*operands)


def exchange(pieces, axis):
    ways = len(pieces)
    return [
        lax.ppermute(piece, axis, [(at, at ^ step) for at in range(ways)]) if step else piece
        for piece, step in zip(pieces, partners(ways))
    ]


def body(field, spec_first, spec_second, spec_third, ffn_in, ffn_out, bias_in, bias_out):
    channels, rows, cols, lanes = field.shape
    ways, col_ways = lax.axis_size("row"), lax.axis_size("col")
    row_me = lax.axis_index("row")
    me = row_me.reshape(1).astype(jnp.int32)
    row_order = row_me ^ jnp.array(partners(ways))
    chunks = cols // ways
    across = rows // col_ways
    ffn = (ffn_in.T, ffn_out.T, bias_in[:, None], bias_out[:, None])

    half = max(1, chunks // 2)
    rest = chunks - half
    early = pack(field, 0, half, ways, me, None)
    late = pack(field, half, rest, ways, me, early[0])
    early_in, late_in = exchange(early, "row"), exchange(late, "row")
    side = rows_first(field, late[0])
    first_mix, second_mix, third_mix = mix_rows(side, spec_first, spec_second, spec_third)
    side = side.reshape(col_ways, across, channels, cols, lanes)
    side = lax.all_to_all(side, "col", split_axis=0, concat_axis=0)

    third = last_branch(field, third_mix, 0, 2, None, None)
    third = last_branch(field, third_mix, 1, 2, third, early_in[-3])
    parts = along_lines(early_in, first_mix, row_order, (0, half))
    back = exchange(parts, "row")
    first = [(back, which) for which in range(half)]
    (second,) = along_lines(side, second_mix, after=parts[0])
    second = lax.all_to_all(second, "col", split_axis=0, concat_axis=0)
    second = second.reshape(rows, cols, channels, lanes)
    for which in range(rest):
        parts = along_lines(late_in, first_mix, row_order, (which, 1))
        first.append((exchange(parts, "row"), 0))

    result = None
    for chunk, (branch, which) in enumerate(first):
        result = cells(field, branch, which, second, third, ffn, chunk, me, result)
    return result


def solution(mesh):
    return jax.shard_map(
        body,
        mesh=mesh,
        in_specs=(P("grp", "row", "col", None), P(), P(), P(), P(), P(), P(), P()),
        out_specs=P("grp", "row", "col", None),
        check_vma=False,
    )
```

```python
import functools
import math

import jax
import jax.numpy as jnp
from jax import lax
from jax.experimental import pallas as pl
from jax.experimental.pallas import tpu as pltpu
from jax.sharding import PartitionSpec as P

MIB = 1024 * 1024
VMEM_BYTES = 62 * MIB
PLAN = {'early': 2,
 'order': 2,
 'last': 1,
 'corner': 'last1',
 'near': 'late0',
 'pins': {'pack1': [['early', 5]],
          'last1': [['side', -1], ['early', 4]],
          'dim2b': [['late', 2]],
          'late0': [['late', 6]],
          'dim2a': [['late', 1]],
          'last0': [['early', 7]]},
 'cost': {'pack0': 0.216,
          'pack1': 60,
          'rows': 21.6,
          'mix': 0.96,
          'last0': 0.324,
          'last1': 60,
          'dim1': 0.132,
          'dim2a': 25.92,
          'dim2b': 120,
          'late0': 120,
          'late1': 1.8,
          'late2': 0.162,
          'ffn0': 1.296,
          'ffn1': 3.6,
          'ffn2': 14.4,
          'ffn3': 36.0},
 'groups': [2]}
SPAN = 4.8
NORMAL = (
    0.147212786,
    -0.00633505354,
    0.000398642281,
    -2.65332237e-05,
    1.74432499e-06,
    -1.09393557e-07,
    5.93270033e-09,
    -2.75892574e-10,
    1.73565533e-11,
    -1.17650118e-12,
    3.52373652e-14,
)


def forward_rows(length, mode_count):
    grid_pos = jnp.arange(length, dtype=jnp.int32)[None, :]
    mode_location = jnp.arange(mode_count, dtype=jnp.int32)[:, None]
    phase = (grid_pos * mode_location % length).astype(jnp.float32) * (2.0 * math.pi / length)
    return jnp.concatenate([jnp.cos(phase), -jnp.sin(phase)], axis=0).astype(jnp.bfloat16)


def inverse_rows(length, mode_count):
    mode_location = jnp.arange(mode_count, dtype=jnp.int32)[:, None]
    grid_pos = jnp.arange(length, dtype=jnp.int32)[None, :]
    phase = (grid_pos * mode_location % length).astype(jnp.float32) * (2.0 * math.pi / length)
    factor = jnp.where(mode_location == 0, 1.0, 2.0).astype(jnp.float32) / length
    return jnp.concatenate(
        [factor * jnp.cos(phase), -factor * jnp.sin(phase)], axis=0
    ).astype(jnp.bfloat16)


def mix_kernel(*refs):
    count = len(refs) // 2
    for spec, out in zip(refs[:count], refs[count:]):
        channels = spec.shape[-1]
        for mode in range(spec.shape[1]):
            real = spec[0, mode].astype(jnp.float32).T
            imag = spec[1, mode].astype(jnp.float32).T
            upper = jnp.concatenate([real, -imag], axis=1)
            lower = jnp.concatenate([imag, real], axis=1)
            out[mode, :channels] = upper.astype(jnp.bfloat16)
            out[mode, channels:] = lower.astype(jnp.bfloat16)


def mix_rows(after, *specs):
    _, mode_count, channels, _ = specs[0].shape
    block = min(8, mode_count)
    kernel, token_specs, token = ordered(mix_kernel, after)
    return pl.pallas_call(
        kernel,
        grid=(mode_count // block,),
        in_specs=token_specs
        + [pl.BlockSpec((2, block, channels, channels), lambda g: (0, g, 0, 0))]
        * len(specs),
        out_specs=[pl.BlockSpec((block, 2 * channels, 2 * channels), lambda g: (g, 0, 0))]
        * len(specs),
        out_shape=[hbm(mode_count, 2 * channels, 2 * channels)] * len(specs),
        compiler_params=pltpu.CompilerParams(vmem_limit_bytes=VMEM_BYTES),
        cost_estimate=cost("mix", 0),
        name="mixing_matrices",
    )(*token, *in_hbm(specs))


def hbm(*shape):
    return pltpu.HBM(shape, jnp.bfloat16)


def in_hbm(arrays):
    return [pltpu.with_memory_space_constraint(array, pltpu.HBM) for array in arrays]


def cost(kernel, size):
    micros = PLAN["cost"].get(kernel, 3.0)
    return pl.CostEstimate(
        flops=int(micros * 1.15e9), bytes_accessed=int(size), transcendentals=0
    )


def ordered(kernel, after):
    if after is None:
        return kernel, [], []
    return (
        lambda _, *refs: kernel(*refs),
        [pl.BlockSpec(memory_space=pl.ANY)],
        in_hbm([after]),
    )


def mm(left, right, dims=(1, 0)):
    return lax.dot_general(
        left, right, (((dims[0],), (dims[1],)), ((), ())), preferred_element_type=jnp.float32
    )


def stack_rows(parts):
    if parts[0].shape[0] % 16 == 0:
        return jnp.concatenate(parts, axis=0)
    return jnp.concatenate([p.astype(jnp.float32) for p in parts], axis=0).astype(jnp.bfloat16)


def partners(ways):
    far = list(range(ways // 2, ways))
    near = list(range(1, ways // 2))
    if PLAN["order"] == 1:
        near.reverse()
    if PLAN["order"] == 2:
        far.reverse()
    return [0] + far + near


def pack_kernel(ways, me_ref, x_ref, *refs):
    outs, wide = refs[:ways], refs[ways]
    channels, rows, _, lanes = x_ref.shape
    wide[...] = x_ref[...].astype(jnp.float32).reshape(channels * rows * ways, lanes)
    for out, step in zip(outs, partners(ways)):
        picked = wide[pl.ds(me_ref[0] ^ step, channels * rows, stride=ways), :]
        out[...] = picked.reshape(channels, rows, lanes).astype(jnp.bfloat16)


def pack(kernel_name, field, first, count, ways, me, after):
    channels, rows, _, lanes = field.shape
    depth = min(16, channels)
    token_specs = [pl.BlockSpec(memory_space=pl.ANY)] * len(after)
    token = in_hbm(after)

    def kernel(me_ref, x_ref, *refs):
        pack_kernel(ways, me_ref, x_ref, *refs[len(token) :])

    return pl.pallas_call(
        kernel,
        grid_spec=pltpu.PrefetchScalarGridSpec(
            num_scalar_prefetch=1,
            grid=(count, channels // depth),
            in_specs=[
                pl.BlockSpec((depth, rows, ways, lanes), lambda k, g, me: (g, 0, first + k, 0))
            ]
            + token_specs,
            out_specs=[pl.BlockSpec((None, depth, rows, lanes), lambda k, g, me: (k, g, 0, 0))]
            * ways,
            scratch_shapes=[pltpu.VMEM((depth * rows * ways, lanes), jnp.float32)],
        ),
        out_shape=[hbm(count, channels, rows, lanes)] * ways,
        compiler_params=pltpu.CompilerParams(vmem_limit_bytes=VMEM_BYTES),
        cost_estimate=cost(kernel_name, 0),
        name="pack_columns",
    )(me, *in_hbm([field]), *token)


def side_kernel(ways, me_ref, *refs):
    for x_ref, out_ref in zip(refs[:ways], refs[-ways:]):
        out_ref[...] = x_ref[...]


def rows_first(field, ways, me, after):
    channels, rows, cols, lanes = field.shape
    across = rows // ways

    def rows_of(step):
        return pl.BlockSpec(
            (channels, None, cols, lanes), lambda r, me: (0, (me[1] ^ step) * across + r, 0, 0)
        )

    return pl.pallas_call(
        functools.partial(side_kernel, ways),
        grid_spec=pltpu.PrefetchScalarGridSpec(
            num_scalar_prefetch=1,
            grid=(across,),
            in_specs=[rows_of(step) for step in partners(ways)]
            + [pl.BlockSpec(memory_space=pl.ANY)],
            out_specs=[
                pl.BlockSpec((None, channels, cols, lanes), lambda r, me: (r, 0, 0, 0))
            ]
            * ways,
        ),
        out_shape=[hbm(across, channels, cols, lanes)] * ways,
        compiler_params=pltpu.CompilerParams(vmem_limit_bytes=VMEM_BYTES),
        cost_estimate=cost("rows", 0),
        name="rows_first",
    )(me, *in_hbm([field] * ways + [after]))


def mix_modes(mix_ref, spectra, mixed):
    mode_count, depth, _ = mix_ref.shape
    channels = depth // 2

    def one(mode, _):
        block = spectra[pl.ds(pl.multiple_of(mode * depth, depth), depth), :].astype(jnp.bfloat16)
        result = mm(mix_ref[mode], block)
        for part in range(2):
            mixed[pl.ds(part * mode_count + mode, channels, stride=2 * mode_count), :] = result[
                part * channels : (part + 1) * channels
            ]
        return 0

    lax.fori_loop(0, mode_count, one, 0, unroll=4)


def keep_spectra(spectra, result, channel, mode_count, channels, lanes):
    for at in range(2):
        for part in range(2):
            spectra[pl.ds(part * channels + channel + at, mode_count, stride=2 * channels), :] = (
                result[part * mode_count : (part + 1) * mode_count, at * lanes : (at + 1) * lanes]
            )


def mixed_pair(mixed, channel, coefs):
    start = pl.multiple_of(channel * coefs, 2 * coefs)
    return jnp.concatenate(
        [mixed[pl.ds(start, coefs), :], mixed[pl.ds(start + coefs, coefs), :]], axis=1
    ).astype(jnp.bfloat16)


def lines_kernel(ways, ft_ref, it_ref, mix_ref, *refs):
    pieces, outs = refs[:ways], refs[ways : 2 * ways]
    spectra, mixed, wide = refs[2 * ways :]
    channels, length, lanes = pieces[0].shape
    mode_count = mix_ref.shape[0]
    total = ways * length

    def forward(pair, _):
        channel = 2 * pair
        right = jnp.concatenate(
            [stack_rows([piece[channel + at] for piece in pieces]) for at in range(2)], axis=1
        )
        keep_spectra(spectra, mm(ft_ref[...], right), channel, mode_count, channels, lanes)
        return 0

    lax.fori_loop(0, channels // 2, forward, 0, unroll=4)
    mix_modes(mix_ref, spectra, mixed)

    def inverse(pair, _):
        channel = 2 * pair
        result = mm(it_ref[...], mixed_pair(mixed, channel, 2 * mode_count))
        for at in range(2):
            wide[pl.ds(channel + at, total, stride=channels), :] = result[
                :, at * lanes : (at + 1) * lanes
            ]
        return 0

    lax.fori_loop(0, channels // 2, inverse, 0, unroll=4)
    for step in range(ways):
        part = wide[pl.ds(step * length * channels, length * channels), :]
        outs[step][...] = part.reshape(length, channels, lanes).astype(jnp.bfloat16)


def along_lines(
    kernel_name, pieces, weights, order, begin, count, after=(), held=(), done=None, full=False
):
    ways = len(pieces)
    several, channels, length, lanes = pieces[0].shape
    mode_count = weights.shape[0]
    total = ways * length
    forward = forward_rows(total, mode_count).reshape(2 * mode_count, ways, length)
    forward = jnp.take(forward, order, axis=1).reshape(2 * mode_count, total)
    back = inverse_rows(total, mode_count).T.reshape(ways, length, 2 * mode_count)
    back = jnp.take(back, order, axis=0).reshape(total, 2 * mode_count)
    whole = lambda shape: pl.BlockSpec(shape, lambda g: (0,) * len(shape))
    elsewhere = pl.BlockSpec(memory_space=pl.ANY)
    put, number = (begin, several) if full else (0, count)
    kept = list(done or ()) + list(held)
    moved = 0 if done else ways
    idle = kept + list(after)
    last = len(idle) + 3 + 2 * ways
    return pl.pallas_call(
        lambda *refs: lines_kernel(ways, *refs[len(idle) : last], *refs[-3:]),
        grid=(count,),
        in_specs=[elsewhere] * len(idle)
        + [whole(forward.shape), whole(back.shape), whole(weights.shape)]
        + [pl.BlockSpec((None, channels, length, lanes), lambda g: (begin + g, 0, 0, 0))] * ways,
        out_specs=[
            pl.BlockSpec((None, length, channels, lanes), lambda g: (put + g, 0, 0, 0))
        ]
        * ways
        + [elsewhere] * len(held),
        out_shape=[hbm(number, length, channels, lanes)] * ways
        + [hbm(*array.shape) for array in held],
        input_output_aliases={at: moved + at for at in range(len(kept))},
        scratch_shapes=[
            pltpu.VMEM((2 * channels * mode_count, lanes), jnp.float32),
            pltpu.VMEM((2 * channels * mode_count, lanes), jnp.float32),
            pltpu.VMEM((total * channels, lanes), jnp.float32),
        ],
        compiler_params=pltpu.CompilerParams(vmem_limit_bytes=VMEM_BYTES),
        cost_estimate=cost(kernel_name, 0),
        name="line_branch",
    )(*in_hbm(idle), forward, back, *in_hbm([weights, *pieces]))


def last_kernel(ft_ref, it_ref, mix_ref, x_ref, out_ref, spectra, mixed, wide):
    channels, rows, cols, length = x_ref.shape
    mode_count = mix_ref.shape[0]
    cells = rows * cols

    def forward(pair, _):
        channel = 2 * pair
        right = jnp.concatenate(
            [x_ref[channel + at].reshape(cells, length) for at in range(2)], axis=0
        )
        keep_spectra(
            spectra, mm(ft_ref[...], right, (1, 1)), channel, mode_count, channels, cells
        )
        return 0

    lax.fori_loop(0, channels // 2, forward, 0, unroll=4)
    mix_modes(mix_ref, spectra, mixed)

    def inverse(pair, _):
        channel = 2 * pair
        result = mm(mixed_pair(mixed, channel, 2 * mode_count), it_ref[...], (0, 0))
        for at in range(2):
            wide[pl.ds(channel + at, cells, stride=channels), :] = result[
                at * cells : (at + 1) * cells
            ]
        return 0

    lax.fori_loop(0, channels // 2, inverse, 0, unroll=4)
    out_ref[...] = wide[...].reshape(rows, cols, channels, length).astype(jnp.bfloat16)


def last_branch(kernel_name, field, weights, part, parts, done, after, held=()):
    channels, rows, cols, length = field.shape
    mode_count = weights.shape[0]
    block = max(1, min(rows // parts, 128 // cols))
    steps = rows // block // parts
    forward, back = forward_rows(length, mode_count), inverse_rows(length, mode_count)
    whole = lambda shape: pl.BlockSpec(shape, lambda g: (0,) * len(shape))
    elsewhere = pl.BlockSpec(memory_space=pl.ANY)
    kept = ([] if done is None else [done]) + list(held)
    moved = 1 if done is None else 0
    idle = kept + list(after)
    return pl.pallas_call(
        lambda *refs: last_kernel(*refs[len(idle) : len(idle) + 5], *refs[-3:]),
        grid=(steps,),
        in_specs=[elsewhere] * len(idle)
        + [
            whole(forward.shape),
            whole(back.shape),
            whole(weights.shape),
            pl.BlockSpec(
                (channels, block, cols, length), lambda g: (0, part * steps + g, 0, 0)
            ),
        ],
        out_specs=[
            pl.BlockSpec((block, cols, channels, length), lambda g: (part * steps + g, 0, 0, 0))
        ]
        + [elsewhere] * len(held),
        out_shape=[hbm(rows, cols, channels, length)] + [hbm(*array.shape) for array in held],
        input_output_aliases={at: moved + at for at in range(len(kept))},
        scratch_shapes=[
            pltpu.VMEM((2 * channels * mode_count, block * cols), jnp.float32),
            pltpu.VMEM((2 * channels * mode_count, block * cols), jnp.float32),
            pltpu.VMEM((block * cols * channels, length), jnp.float32),
        ],
        compiler_params=pltpu.CompilerParams(vmem_limit_bytes=VMEM_BYTES),
        cost_estimate=cost(kernel_name, 0),
        name="last_branch",
    )(*in_hbm(idle), forward, back, *in_hbm([weights, field]))


def gelu(x):
    near = jnp.clip(x, -SPAN, SPAN)
    square = near * near - SPAN * SPAN / 2
    ratio = NORMAL[-1] * square + NORMAL[-2]
    for factor in NORMAL[-3::-1]:
        ratio = ratio * square + factor
    return x * (0.5 + near * ratio)


def cell_kernel(ways, col_ways, me_ref, x_ref, win_ref, wout_ref, bin_ref, bout_ref, *refs):
    first, second = refs[:ways], refs[ways : ways + col_ways]
    third = refs[ways + col_ways]
    out_ref, now, wide, before, hidden = refs[-5:]
    channels, rows, _, lanes = x_ref.shape
    steps = partners(ways)

    for place in range(col_ways):

        @pl.when(pl.program_id(0) == place)
        def _():
            now[...] = second[place][...]

    def one(row, _):
        for place in range(0, ways, 2):
            summed = []
            for at in range(2):
                col = me_ref[0] ^ steps[place + at]
                pair = first[place + at][row].astype(jnp.float32)
                pair = (pair + now[row, col].astype(jnp.float32)).astype(jnp.bfloat16)
                total = pair.astype(jnp.float32) + third[row, col].astype(jnp.float32)
                summed.append(total.astype(jnp.bfloat16))
            before[...] = mm(win_ref[...], jnp.concatenate(summed, axis=1))
            for start in range(0, before.shape[0], 32):
                units = pl.ds(start, 32)
                hidden[units] = gelu(before[units] + bin_ref[units]).astype(jnp.bfloat16)
            result = mm(wout_ref[...], hidden[...]) + bout_ref[...]
            for at in range(2):
                col = me_ref[0] ^ steps[place + at]
                wide[pl.ds(col, channels, stride=ways), :] = result[
                    :, at * lanes : (at + 1) * lanes
                ]
        total = wide[...].reshape(channels, ways, lanes) + x_ref[:, row].astype(jnp.float32)
        out_ref[:, row] = total.astype(jnp.bfloat16)
        return 0

    lax.fori_loop(0, rows, one, 0)


def cells(field, first, which, second, third, ffn, chunk, me, done, after):
    channels, rows, cols, lanes = field.shape
    ways, col_ways = len(first), len(second)
    across = rows // col_ways
    steps = partners(col_ways)

    def block(place, me):
        step = steps[0]
        for other in range(1, col_ways):
            step = jnp.where(place == other, steps[other], step)
        return me[1] ^ step

    whole = lambda shape: pl.BlockSpec(shape, lambda *_: (0,) * len(shape))
    tile = pl.BlockSpec(
        (channels, across, ways, lanes), lambda p, me: (0, block(p, me), chunk, 0)
    )
    in_specs = [tile] + [whole(w.shape) for w in ffn]
    in_specs += [
        pl.BlockSpec((None, across, channels, lanes), lambda p, me: (which, block(p, me), 0, 0))
    ] * ways
    in_specs += [
        pl.BlockSpec((across, ways, channels, lanes), lambda p, me: (0, chunk, 0, 0))
    ] * col_ways
    in_specs.append(
        pl.BlockSpec((across, ways, channels, lanes), lambda p, me: (block(p, me), chunk, 0, 0))
    )
    operands = [me, *in_hbm([field]), *ffn, *in_hbm([*first, *second, third])]
    aliases = {}
    if done is not None:
        aliases = {len(operands): 0}
    for array in (done, after):
        if array is not None:
            in_specs.append(pl.BlockSpec(memory_space=pl.ANY))
            operands += in_hbm([array])
    return pl.pallas_call(
        functools.partial(cell_kernel, ways, col_ways),
        grid_spec=pltpu.PrefetchScalarGridSpec(
            num_scalar_prefetch=1,
            grid=(col_ways,),
            in_specs=in_specs,
            out_specs=tile,
            scratch_shapes=[
                pltpu.VMEM((across, ways, channels, lanes), jnp.bfloat16),
                pltpu.VMEM((channels * ways, lanes), jnp.float32),
                pltpu.VMEM((ffn[0].shape[0], 2 * lanes), jnp.float32),
                pltpu.VMEM((ffn[0].shape[0], 2 * lanes), jnp.bfloat16),
            ],
        ),
        out_shape=hbm(*field.shape),
        input_output_aliases=aliases,
        compiler_params=pltpu.CompilerParams(vmem_limit_bytes=VMEM_BYTES),
        cost_estimate=cost(f"ffn{chunk}", 0),
        name="feed_forward",
    )(*operands)


def exchange(pieces, axis, skip=None, only=None):
    ways = len(pieces)
    got = list(pieces)
    for place, step in enumerate(partners(ways)):
        if step and place != skip and only in (None, place):
            pairs = [(at, at ^ step) for at in range(ways)]
            got[place] = lax.ppermute(pieces[place], axis, pairs)
    return got


def body(field, spec_first, spec_second, spec_third, ffn_in, ffn_out, bias_in, bias_out):
    channels, rows, cols, lanes = field.shape
    ways, col_ways = lax.axis_size("row"), lax.axis_size("col")
    row_me, col_me = lax.axis_index("row"), lax.axis_index("col")
    me = jnp.stack([row_me, col_me]).astype(jnp.int32)
    row_order = row_me ^ jnp.array(partners(ways))
    col_order = col_me ^ jnp.array(partners(col_ways))
    chunks = cols // ways
    across = rows // col_ways
    ffn = (ffn_in.T, ffn_out.T, bias_in[:, None], bias_out[:, None])

    early_count = max(1, min(PLAN["early"], chunks - 1))
    rest = chunks - early_count
    nearest = ways // 2 + 1
    seen = {}

    def pins(kernel):
        return [seen[name][place] for name, place in PLAN["pins"].get(kernel, ())]

    early = pack("pack0", field, 0, early_count, ways, me, [])
    seen["early"] = early_in = exchange(early, "row")
    late = pack("pack1", field, early_count, rest, ways, me, [early[0]] + pins("pack1"))
    seen["late"] = late_in = exchange(late, "row")
    corner = 2
    side = list(rows_first(field, col_ways, me, late[0]))
    seen["side"] = side_in = exchange(side, "col", skip=corner)
    first_mix, second_mix, third_mix = mix_rows(side[0], spec_first, spec_second, spec_third)

    def last(part, done, after):
        name = f"last{part}"
        held = [side[corner]] if PLAN["corner"] == name else []
        got = last_branch(name, field, third_mix, part, 2, done, after + pins(name), held)
        if held:
            side[corner] = got[1]
        return got[0]

    third = last(0, None, [])
    if PLAN["last"] == 0:
        third = last(1, third, [])
    side_in[corner] = exchange(side, "col", only=corner)[corner]
    parts = along_lines(
        "dim1", early_in, first_mix, row_order, 0, early_count, after=[third] + pins("dim1")
    )
    token = parts[0]
    if PLAN["last"] == 1:
        third = last(1, third, [token])
        token = third
    cut = across // 2
    second = along_lines(
        "dim2a", side_in, second_mix, col_order, 0, cut, [token] + pins("dim2a"), full=True
    )
    token = second[0]
    if PLAN["last"] == 2:
        third = last(1, third, [token])
        token = third
    second = along_lines(
        "dim2b",
        side_in,
        second_mix,
        col_order,
        cut,
        across - cut,
        [token] + pins("dim2b"),
        done=second,
        full=True,
    )
    token = second[0]
    seen["second"] = second_in = exchange(second, "col")
    if PLAN["last"] == 3:
        third = last(1, third, [token])
        token = third
    late_parts, near, begin = [], parts[nearest:], 0
    groups = PLAN["groups"] if sum(PLAN["groups"]) == rest else [1] * rest
    for at, count in enumerate(groups):
        name = f"late{at}"
        held = near if PLAN["near"] == name else []
        got = along_lines(
            name, late_in, first_mix, row_order, begin, count, [token] + pins(name), held=held
        )
        begin += count
        late_parts.append((got[:ways], count))
        near = got[ways:] if held else near
        token = got[0]
    if PLAN["last"] == 4:
        third = last(1, third, [token])
        token = third
    seen["back"] = back = exchange(parts[:nearest] + near, "row")
    first = [(back, which) for which in range(early_count)]
    for got, count in late_parts:
        back = exchange(got, "row")
        first += [(back, which) for which in range(count)]

    result = None
    for chunk, (branch, which) in enumerate(first):
        result = cells(
            field, branch, which, second_in, third, ffn, chunk, me, result, token
        )
        token = None
    return result


def solution(mesh):
    return jax.shard_map(
        body,
        mesh=mesh,
        in_specs=(P("grp", "row", "col", None), P(), P(), P(), P(), P(), P(), P()),
        out_specs=P("grp", "row", "col", None),
        check_vma=False,
    )
```

```python
import functools
import math

import jax
import jax.numpy as jnp
from jax import lax
from jax.experimental import pallas as pl
from jax.experimental.pallas import tpu as pltpu
from jax.sharding import PartitionSpec as P

MIB = 1024 * 1024
VMEM_BYTES = 62 * MIB
PLAN = {
    "early": 2,
    "groups": [1, 1],
    "last": 0,
    "corner": "",
    "pins": {"last1": [("side", -1)]},
    "cost": {"pack0": 8.0, "pack1": 8.0, "rows": 7.6, "mix": 5.0, "last0": 22.0, "last1": 22.0, "dim1": 20.0, "dim2a": 20.0, "dim2b": 20.0, "late0": 10.0, "late1": 10.0, "ffn0": 21.0, "ffn1": 21.0, "ffn2": 21.0, "ffn3": 21.0},
}
HALF_ROOT = math.sqrt(0.5)


def forward_rows(length, mode_count):
    grid_pos = jnp.arange(length, dtype=jnp.int32)[None, :]
    mode_location = jnp.arange(mode_count, dtype=jnp.int32)[:, None]
    phase = (grid_pos * mode_location % length).astype(jnp.float32) * (2.0 * math.pi / length)
    return jnp.concatenate([jnp.cos(phase), -jnp.sin(phase)], axis=0).astype(jnp.bfloat16)


def inverse_rows(length, mode_count):
    mode_location = jnp.arange(mode_count, dtype=jnp.int32)[:, None]
    grid_pos = jnp.arange(length, dtype=jnp.int32)[None, :]
    phase = (grid_pos * mode_location % length).astype(jnp.float32) * (2.0 * math.pi / length)
    factor = jnp.where(mode_location == 0, 1.0, 2.0).astype(jnp.float32) / length
    return jnp.concatenate(
        [factor * jnp.cos(phase), -factor * jnp.sin(phase)], axis=0
    ).astype(jnp.bfloat16)


def mix_kernel(*refs):
    count = len(refs) // 2
    for spec, out in zip(refs[:count], refs[count:]):
        channels = spec.shape[-1]
        for mode in range(spec.shape[1]):
            real = spec[0, mode].astype(jnp.float32).T
            imag = spec[1, mode].astype(jnp.float32).T
            upper = jnp.concatenate([real, -imag], axis=1)
            lower = jnp.concatenate([imag, real], axis=1)
            out[mode, :channels] = upper.astype(jnp.bfloat16)
            out[mode, channels:] = lower.astype(jnp.bfloat16)


def mix_rows(after, *specs):
    _, mode_count, channels, _ = specs[0].shape
    block = min(8, mode_count)
    kernel, token_specs, token = ordered(mix_kernel, after)
    return pl.pallas_call(
        kernel,
        grid=(mode_count // block,),
        in_specs=token_specs
        + [pl.BlockSpec((2, block, channels, channels), lambda g: (0, g, 0, 0))]
        * len(specs),
        out_specs=[pl.BlockSpec((block, 2 * channels, 2 * channels), lambda g: (g, 0, 0))]
        * len(specs),
        out_shape=[hbm(mode_count, 2 * channels, 2 * channels)] * len(specs),
        compiler_params=pltpu.CompilerParams(vmem_limit_bytes=VMEM_BYTES),
        cost_estimate=cost("mix", 0),
        name="mixing_matrices",
    )(*token, *in_hbm(specs))


def hbm(*shape):
    return pltpu.HBM(shape, jnp.bfloat16)


def in_hbm(arrays):
    return [pltpu.with_memory_space_constraint(array, pltpu.HBM) for array in arrays]


def cost(kernel, size):
    micros = PLAN["cost"].get(kernel, 3.0)
    return pl.CostEstimate(
        flops=int(micros * 1.15e9), bytes_accessed=int(size), transcendentals=0
    )


def ordered(kernel, after):
    if after is None:
        return kernel, [], []
    return (
        lambda _, *refs: kernel(*refs),
        [pl.BlockSpec(memory_space=pl.ANY)],
        in_hbm([after]),
    )


def mm(left, right, dims=(1, 0)):
    return lax.dot_general(
        left, right, (((dims[0],), (dims[1],)), ((), ())), preferred_element_type=jnp.float32
    )


def stack_rows(parts):
    if parts[0].shape[0] % 16 == 0:
        return jnp.concatenate(parts, axis=0)
    return jnp.concatenate([p.astype(jnp.float32) for p in parts], axis=0).astype(jnp.bfloat16)


def pack_kernel(x_ref, *refs):
    out_ref, wide = refs[-2:]
    channels, rows, ways, lanes = x_ref.shape
    wide[...] = x_ref[...].astype(jnp.float32).reshape(channels * rows * ways, lanes)
    for way in range(ways):
        picked = wide[pl.ds(way, channels * rows, stride=ways), :]
        out_ref[way] = picked.reshape(channels, rows, lanes).astype(jnp.bfloat16)


def pack(kernel_name, field, first, count, ways, after):
    channels, rows, _, lanes = field.shape
    depth = min(16, channels)
    return pl.pallas_call(
        pack_kernel,
        grid=(count, channels // depth),
        in_specs=[pl.BlockSpec((depth, rows, ways, lanes), lambda k, g: (g, 0, first + k, 0))]
        + [pl.BlockSpec(memory_space=pl.ANY)] * len(after),
        out_specs=pl.BlockSpec((ways, None, depth, rows, lanes), lambda k, g: (0, k, g, 0, 0)),
        out_shape=hbm(ways, count, channels, rows, lanes),
        scratch_shapes=[pltpu.VMEM((depth * rows * ways, lanes), jnp.float32)],
        compiler_params=pltpu.CompilerParams(vmem_limit_bytes=VMEM_BYTES),
        cost_estimate=cost(kernel_name, 0),
        name="pack_columns",
    )(*in_hbm([field, *after]))


def side_kernel(ways, me_ref, *refs):
    for x_ref, out_ref in zip(refs[:ways], refs[-ways:]):
        out_ref[...] = x_ref[...]


def rows_first(field, ways, me, after):
    channels, rows, cols, lanes = field.shape
    across = rows // ways

    def rows_of(step):
        return pl.BlockSpec(
            (channels, None, cols, lanes), lambda r, me: (0, (me[1] ^ step) * across + r, 0, 0)
        )

    return pl.pallas_call(
        functools.partial(side_kernel, ways),
        grid_spec=pltpu.PrefetchScalarGridSpec(
            num_scalar_prefetch=1,
            grid=(across,),
            in_specs=[rows_of(step) for step in range(ways)]
            + [pl.BlockSpec(memory_space=pl.ANY)],
            out_specs=[
                pl.BlockSpec((None, channels, cols, lanes), lambda r, me: (r, 0, 0, 0))
            ]
            * ways,
        ),
        out_shape=[hbm(across, channels, cols, lanes)] * ways,
        compiler_params=pltpu.CompilerParams(vmem_limit_bytes=VMEM_BYTES),
        cost_estimate=cost("rows", 0),
        name="rows_first",
    )(me, *in_hbm([field] * ways + [after]))


def mix_modes(mix_ref, spectra, mixed):
    mode_count, depth, _ = mix_ref.shape
    channels = depth // 2

    def one(mode, _):
        block = spectra[pl.ds(pl.multiple_of(mode * depth, depth), depth), :].astype(jnp.bfloat16)
        result = mm(mix_ref[mode], block)
        for part in range(2):
            mixed[pl.ds(part * mode_count + mode, channels, stride=2 * mode_count), :] = result[
                part * channels : (part + 1) * channels
            ]
        return 0

    lax.fori_loop(0, mode_count, one, 0, unroll=4)


def keep_spectra(spectra, result, channel, mode_count, channels, lanes):
    for at in range(2):
        for part in range(2):
            spectra[pl.ds(part * channels + channel + at, mode_count, stride=2 * channels), :] = (
                result[part * mode_count : (part + 1) * mode_count, at * lanes : (at + 1) * lanes]
            )


def mixed_pair(mixed, channel, coefs):
    start = pl.multiple_of(channel * coefs, 2 * coefs)
    return jnp.concatenate(
        [mixed[pl.ds(start, coefs), :], mixed[pl.ds(start + coefs, coefs), :]], axis=1
    ).astype(jnp.bfloat16)


def lines_kernel(ways, ft_ref, it_ref, mix_ref, *refs):
    refs, (spectra, mixed, wide) = refs[:-3], refs[-3:]
    count = len(refs) // 2
    pieces, outs = refs[:count], refs[count:]
    if count < ways:
        pieces = [pieces[0].at[way] for way in range(ways)]
        outs = [outs[0].at[way] for way in range(ways)]
    channels, length, lanes = pieces[0].shape
    mode_count = mix_ref.shape[0]
    total = ways * length

    def forward(pair, _):
        channel = 2 * pair
        right = jnp.concatenate(
            [stack_rows([piece[channel + at] for piece in pieces]) for at in range(2)], axis=1
        )
        keep_spectra(spectra, mm(ft_ref[...], right), channel, mode_count, channels, lanes)
        return 0

    lax.fori_loop(0, channels // 2, forward, 0, unroll=4)
    mix_modes(mix_ref, spectra, mixed)

    def inverse(pair, _):
        channel = 2 * pair
        result = mm(it_ref[...], mixed_pair(mixed, channel, 2 * mode_count))
        for at in range(2):
            wide[pl.ds(channel + at, total, stride=channels), :] = result[
                :, at * lanes : (at + 1) * lanes
            ]
        return 0

    lax.fori_loop(0, channels // 2, inverse, 0, unroll=4)
    for step in range(ways):
        part = wide[pl.ds(step * length * channels, length * channels), :]
        outs[step][...] = part.reshape(length, channels, lanes).astype(jnp.bfloat16)


def along_lines(kernel_name, pieces, weights, me, begin, count, after, done=None):
    stacked = not isinstance(pieces, list)
    if stacked:
        ways, several, channels, length, lanes = pieces.shape
        pieces = [pieces]
    else:
        ways = len(pieces)
        several, channels, length, lanes = pieces[0].shape
    mode_count = weights.shape[0]
    total = ways * length
    forward = forward_rows(total, mode_count)
    back = inverse_rows(total, mode_count).T
    if stacked:
        in_spec = pl.BlockSpec(
            (ways, None, channels, length, lanes), lambda g: (0, begin + g, 0, 0, 0)
        )
        out_spec = pl.BlockSpec((ways, None, length, channels, lanes), lambda g: (0, g, 0, 0, 0))
        out_shape = hbm(ways, count, length, channels, lanes)
    else:
        order = me ^ jnp.arange(ways)
        forward = forward.reshape(2 * mode_count, ways, length)
        forward = jnp.take(forward, order, axis=1).reshape(2 * mode_count, total)
        back = back.reshape(ways, length, 2 * mode_count)
        back = jnp.take(back, order, axis=0).reshape(total, 2 * mode_count)
        in_spec = pl.BlockSpec((None, channels, length, lanes), lambda g: (begin + g, 0, 0, 0))
        out_spec = pl.BlockSpec((None, length, channels, lanes), lambda g: (begin + g, 0, 0, 0))
        out_shape = hbm(several, length, channels, lanes)
    whole = lambda shape: pl.BlockSpec(shape, lambda g: (0,) * len(shape))
    kept = list(done or ())
    idle = kept + list(after)
    return pl.pallas_call(
        lambda *refs: lines_kernel(ways, *refs[len(idle) :]),
        grid=(count,),
        in_specs=[pl.BlockSpec(memory_space=pl.ANY)] * len(idle)
        + [whole(forward.shape), whole(back.shape), whole(weights.shape)]
        + [in_spec] * len(pieces),
        out_specs=[out_spec] * len(pieces),
        out_shape=[out_shape] * len(pieces),
        input_output_aliases={at: at for at in range(len(kept))},
        scratch_shapes=[
            pltpu.VMEM((2 * channels * mode_count, lanes), jnp.float32),
            pltpu.VMEM((2 * channels * mode_count, lanes), jnp.float32),
            pltpu.VMEM((total * channels, lanes), jnp.float32),
        ],
        compiler_params=pltpu.CompilerParams(vmem_limit_bytes=VMEM_BYTES),
        cost_estimate=cost(kernel_name, 0),
        name="line_branch",
    )(*in_hbm(idle), forward, back, *in_hbm([weights, *pieces]))


def last_kernel(ft_ref, it_ref, mix_ref, x_ref, out_ref, spectra, mixed, wide):
    channels, rows, cols, length = x_ref.shape
    mode_count = mix_ref.shape[0]
    cells = rows * cols

    def forward(pair, _):
        channel = 2 * pair
        right = jnp.concatenate(
            [x_ref[channel + at].reshape(cells, length) for at in range(2)], axis=0
        )
        keep_spectra(
            spectra, mm(ft_ref[...], right, (1, 1)), channel, mode_count, channels, cells
        )
        return 0

    lax.fori_loop(0, channels // 2, forward, 0, unroll=4)
    mix_modes(mix_ref, spectra, mixed)

    def inverse(pair, _):
        channel = 2 * pair
        result = mm(mixed_pair(mixed, channel, 2 * mode_count), it_ref[...], (0, 0))
        for at in range(2):
            wide[pl.ds(channel + at, cells, stride=channels), :] = result[
                at * cells : (at + 1) * cells
            ]
        return 0

    lax.fori_loop(0, channels // 2, inverse, 0, unroll=4)
    out_ref[...] = wide[...].reshape(rows, cols, channels, length).astype(jnp.bfloat16)


def last_branch(kernel_name, field, weights, part, parts, done, after, held=()):
    channels, rows, cols, length = field.shape
    mode_count = weights.shape[0]
    block = max(1, min(rows // parts, 128 // cols))
    steps = rows // block // parts
    forward, back = forward_rows(length, mode_count), inverse_rows(length, mode_count)
    whole = lambda shape: pl.BlockSpec(shape, lambda g: (0,) * len(shape))
    elsewhere = pl.BlockSpec(memory_space=pl.ANY)
    kept = ([] if done is None else [done]) + list(held)
    moved = 1 if done is None else 0
    idle = kept + list(after)
    return pl.pallas_call(
        lambda *refs: last_kernel(*refs[len(idle) : len(idle) + 5], *refs[-3:]),
        grid=(steps,),
        in_specs=[elsewhere] * len(idle)
        + [
            whole(forward.shape),
            whole(back.shape),
            whole(weights.shape),
            pl.BlockSpec(
                (channels, block, cols, length), lambda g: (0, part * steps + g, 0, 0)
            ),
        ],
        out_specs=[
            pl.BlockSpec((block, cols, channels, length), lambda g: (part * steps + g, 0, 0, 0))
        ]
        + [elsewhere] * len(held),
        out_shape=[hbm(rows, cols, channels, length)] + [hbm(*array.shape) for array in held],
        input_output_aliases={at: moved + at for at in range(len(kept))},
        scratch_shapes=[
            pltpu.VMEM((2 * channels * mode_count, block * cols), jnp.float32),
            pltpu.VMEM((2 * channels * mode_count, block * cols), jnp.float32),
            pltpu.VMEM((block * cols * channels, length), jnp.float32),
        ],
        compiler_params=pltpu.CompilerParams(vmem_limit_bytes=VMEM_BYTES),
        cost_estimate=cost(kernel_name, 0),
        name="last_branch",
    )(*in_hbm(idle), forward, back, *in_hbm([weights, field]))


def cell_kernel(col_ways, me_ref, x_ref, win_ref, wout_ref, bin_ref, bout_ref, *refs):
    first_ref, second, third_ref = refs[0], refs[1 : 1 + col_ways], refs[1 + col_ways]
    out_ref, now, wide = refs[-3:]
    channels, _, ways, lanes = x_ref.shape

    for step in range(col_ways):

        @pl.when(pl.program_id(0) == step)
        def _():
            now[...] = second[step][...]

    for col in range(0, ways, 2):
        summed = []
        for at in range(2):
            pair = first_ref[col + at].astype(jnp.float32) + now[col + at].astype(jnp.float32)
            pair = pair.astype(jnp.bfloat16).astype(jnp.float32)
            total = pair + third_ref[col + at].astype(jnp.float32)
            summed.append(total.astype(jnp.bfloat16))
        pre = mm(win_ref[...], jnp.concatenate(summed, axis=1)) + bin_ref[...]
        hidden = (0.5 * pre * (1.0 + lax.erf(pre * HALF_ROOT))).astype(jnp.bfloat16)
        result = mm(wout_ref[...], hidden) + bout_ref[...]
        for at in range(2):
            wide[pl.ds(col + at, channels, stride=ways), :] = result[
                :, at * lanes : (at + 1) * lanes
            ]
    total = wide[...].reshape(channels, ways, lanes) + x_ref[:, 0].astype(jnp.float32)
    out_ref[:, 0] = total.astype(jnp.bfloat16)


def cells(field, first, which, second, third, ffn, chunk, me, done, after):
    channels, rows, cols, lanes = field.shape
    ways, col_ways = first.shape[0], len(second)
    across = rows // col_ways

    def row(step, at, me):
        return (me[1] ^ step) * across + at

    def own_row(which):
        def index(step, at, me):
            now = jnp.where(step == which, at, jnp.where(step < which, 0, across - 1))
            return now, chunk, 0, 0

        return pl.BlockSpec((None, ways, channels, lanes), index)

    whole = lambda shape: pl.BlockSpec(shape, lambda *_: (0,) * len(shape))
    tile = pl.BlockSpec((channels, 1, ways, lanes), lambda s, a, me: (0, row(s, a, me), chunk, 0))
    in_specs = [tile] + [whole(w.shape) for w in ffn]
    in_specs.append(
        pl.BlockSpec(
            (ways, None, None, channels, lanes),
            lambda s, a, me: (0, which, row(s, a, me), 0, 0),
        )
    )
    in_specs += [own_row(step) for step in range(col_ways)]
    in_specs.append(
        pl.BlockSpec((None, ways, channels, lanes), lambda s, a, me: (row(s, a, me), chunk, 0, 0))
    )
    operands = [me, *in_hbm([field]), *ffn, *in_hbm([first, *second, third])]
    aliases = {}
    if done is not None:
        aliases = {len(operands): 0}
    for array in (done, after):
        if array is not None:
            in_specs.append(pl.BlockSpec(memory_space=pl.ANY))
            operands += in_hbm([array])
    return pl.pallas_call(
        functools.partial(cell_kernel, col_ways),
        grid_spec=pltpu.PrefetchScalarGridSpec(
            num_scalar_prefetch=1,
            grid=(col_ways, across),
            in_specs=in_specs,
            out_specs=tile,
            scratch_shapes=[
                pltpu.VMEM((ways, channels, lanes), jnp.bfloat16),
                pltpu.VMEM((channels * ways, lanes), jnp.float32),
            ],
        ),
        out_shape=hbm(*field.shape),
        input_output_aliases=aliases,
        compiler_params=pltpu.CompilerParams(vmem_limit_bytes=VMEM_BYTES),
        cost_estimate=cost(f"ffn{chunk}", 0),
        name="feed_forward",
    )(*operands)


def swap(piece, axis, step):
    ways = lax.axis_size(axis)
    return lax.ppermute(piece, axis, [(at, at ^ step) for at in range(ways)])


def exchange(pieces, axis, skip=None):
    return [
        swap(piece, axis, step) if step not in (0, skip) else piece
        for step, piece in enumerate(pieces)
    ]


def trade(stack):
    return lax.all_to_all(stack, "row", split_axis=0, concat_axis=0)


def body(field, spec_first, spec_second, spec_third, ffn_in, ffn_out, bias_in, bias_out):
    channels, rows, cols, lanes = field.shape
    ways, col_ways = lax.axis_size("row"), lax.axis_size("col")
    row_me, col_me = lax.axis_index("row"), lax.axis_index("col")
    me = jnp.stack([row_me, col_me]).astype(jnp.int32)
    chunks = cols // ways
    across = rows // col_ways
    ffn = (ffn_in.T, ffn_out.T, bias_in[:, None], bias_out[:, None])

    early_count = max(1, min(PLAN["early"], chunks - 1))
    rest = chunks - early_count
    seen = {}

    def pins(kernel):
        return [seen[name][place] for name, place in PLAN["pins"].get(kernel, ())]

    early = pack("pack0", field, 0, early_count, ways, [])
    early_in = trade(early)
    late = pack("pack1", field, early_count, rest, ways, [early])
    late_in = trade(late)
    seen["early"], seen["late"] = [early_in], [late_in]
    corner = 3
    side = list(rows_first(field, col_ways, me, early))
    seen["side"] = side_in = exchange(side, "col", skip=corner)
    first_mix, second_mix, third_mix = mix_rows(side[0], spec_first, spec_second, spec_third)

    def last(part, done, after):
        name = f"last{part}"
        held = [side[corner]] if PLAN["corner"] == name else []
        got = last_branch(name, field, third_mix, part, 2, done, after + pins(name), held)
        if held:
            side[corner] = got[1]
        return got[0]

    third = last(0, None, [])
    if PLAN["last"] == 0:
        third = last(1, third, [])
    side_in[corner] = swap(side[corner], "col", corner)
    parts = along_lines(
        "dim1", early_in, first_mix, None, 0, early_count, [third] + pins("dim1")
    )[0]
    back = [(trade(parts), early_count)]
    token = parts
    if PLAN["last"] == 1:
        third = last(1, third, [token])
        token = third
    cut = across // 2
    second = along_lines(
        "dim2a", side_in, second_mix, col_me, 0, cut, [token] + pins("dim2a")
    )
    token = second[0]
    if PLAN["last"] == 2:
        third = last(1, third, [token])
        token = third
    second = along_lines(
        "dim2b",
        side_in,
        second_mix,
        col_me,
        cut,
        across - cut,
        [token] + pins("dim2b"),
        done=second,
    )
    token = second[0]
    second_in = exchange(second, "col")
    seen["second"] = second_in
    if PLAN["last"] == 3:
        third = last(1, third, [token])
        token = third
    groups = PLAN["groups"] if sum(PLAN["groups"]) == rest else [1] * rest
    begin = 0
    for at, count in enumerate(groups):
        name = f"late{at}"
        parts = along_lines(name, late_in, first_mix, None, begin, count, [token] + pins(name))[0]
        back.append((trade(parts), count))
        begin += count
        token = parts
    if PLAN["last"] == 4:
        third = last(1, third, [token])
        token = third

    result, chunk = None, 0
    for branch, count in back:
        for which in range(count):
            result = cells(
                field, branch, which, second_in, third, ffn, chunk, me, result, token
            )
            chunk, token = chunk + 1, None
    return result


def solution(mesh):
    return jax.shard_map(
        body,
        mesh=mesh,
        in_specs=(P("grp", "row", "col", None), P(), P(), P(), P(), P(), P(), P()),
        out_specs=P("grp", "row", "col", None),
        check_vma=False,
    )
```

```python
import functools
import math

import jax
import jax.numpy as jnp
from jax import lax
from jax.experimental import pallas as pl
from jax.experimental.pallas import tpu as pltpu
from jax.sharding import PartitionSpec as P

MIB = 1024 * 1024
VMEM_BYTES = 62 * MIB
PLAN = {
    "early": 1,
    "groups": [2, 1],
    "last": 0,
    "corner": "",
    "pins": {"last1": [("side", -1)]},
    "cost": {"pack0": 4.0, "pack1": 11.0, "rows": 7.6, "mix": 5.0, "last0": 22.0, "last1": 22.0, "dim1": 10.0, "dim2a": 20.0, "dim2b": 20.0, "late0": 20.0, "late1": 10.0, "ffn0": 21.0, "ffn1": 21.0, "ffn2": 21.0, "ffn3": 21.0},
}
HALF_ROOT = math.sqrt(0.5)


def forward_rows(length, mode_count):
    grid_pos = jnp.arange(length, dtype=jnp.int32)[None, :]
    mode_location = jnp.arange(mode_count, dtype=jnp.int32)[:, None]
    phase = (grid_pos * mode_location % length).astype(jnp.float32) * (2.0 * math.pi / length)
    return jnp.concatenate([jnp.cos(phase), -jnp.sin(phase)], axis=0).astype(jnp.bfloat16)


def inverse_rows(length, mode_count):
    mode_location = jnp.arange(mode_count, dtype=jnp.int32)[:, None]
    grid_pos = jnp.arange(length, dtype=jnp.int32)[None, :]
    phase = (grid_pos * mode_location % length).astype(jnp.float32) * (2.0 * math.pi / length)
    factor = jnp.where(mode_location == 0, 1.0, 2.0).astype(jnp.float32) / length
    return jnp.concatenate(
        [factor * jnp.cos(phase), -factor * jnp.sin(phase)], axis=0
    ).astype(jnp.bfloat16)


def mix_kernel(*refs):
    count = len(refs) // 2
    for spec, out in zip(refs[:count], refs[count:]):
        channels = spec.shape[-1]
        for mode in range(spec.shape[1]):
            real = spec[0, mode].astype(jnp.float32).T
            imag = spec[1, mode].astype(jnp.float32).T
            upper = jnp.concatenate([real, -imag], axis=1)
            lower = jnp.concatenate([imag, real], axis=1)
            out[mode, :channels] = upper.astype(jnp.bfloat16)
            out[mode, channels:] = lower.astype(jnp.bfloat16)


def mix_rows(after, *specs):
    _, mode_count, channels, _ = specs[0].shape
    block = min(8, mode_count)
    kernel, token_specs, token = ordered(mix_kernel, after)
    return pl.pallas_call(
        kernel,
        grid=(mode_count // block,),
        in_specs=token_specs
        + [pl.BlockSpec((2, block, channels, channels), lambda g: (0, g, 0, 0))]
        * len(specs),
        out_specs=[pl.BlockSpec((block, 2 * channels, 2 * channels), lambda g: (g, 0, 0))]
        * len(specs),
        out_shape=[hbm(mode_count, 2 * channels, 2 * channels)] * len(specs),
        compiler_params=pltpu.CompilerParams(vmem_limit_bytes=VMEM_BYTES),
        cost_estimate=cost("mix", 0),
        name="mixing_matrices",
    )(*token, *in_hbm(specs))


def hbm(*shape):
    return pltpu.HBM(shape, jnp.bfloat16)


def in_hbm(arrays):
    return [pltpu.with_memory_space_constraint(array, pltpu.HBM) for array in arrays]


def cost(kernel, size):
    micros = PLAN["cost"].get(kernel, 3.0)
    return pl.CostEstimate(
        flops=int(micros * 1.15e9), bytes_accessed=int(size), transcendentals=0
    )


def ordered(kernel, after):
    if after is None:
        return kernel, [], []
    return (
        lambda _, *refs: kernel(*refs),
        [pl.BlockSpec(memory_space=pl.ANY)],
        in_hbm([after]),
    )


def mm(left, right, dims=(1, 0)):
    return lax.dot_general(
        left, right, (((dims[0],), (dims[1],)), ((), ())), preferred_element_type=jnp.float32
    )


def stack_rows(parts):
    if parts[0].shape[0] % 16 == 0:
        return jnp.concatenate(parts, axis=0)
    return jnp.concatenate([p.astype(jnp.float32) for p in parts], axis=0).astype(jnp.bfloat16)


def pack_kernel(x_ref, *refs):
    out_ref, wide = refs[-2:]
    channels, rows, ways, lanes = x_ref.shape
    wide[...] = x_ref[...].astype(jnp.float32).reshape(channels * rows * ways, lanes)
    for way in range(ways):
        picked = wide[pl.ds(way, channels * rows, stride=ways), :]
        out_ref[way] = picked.reshape(channels, rows, lanes).astype(jnp.bfloat16)


def pack(kernel_name, field, first, count, ways, after):
    channels, rows, _, lanes = field.shape
    depth = min(16, channels)
    return pl.pallas_call(
        pack_kernel,
        grid=(count, channels // depth),
        in_specs=[pl.BlockSpec((depth, rows, ways, lanes), lambda k, g: (g, 0, first + k, 0))]
        + [pl.BlockSpec(memory_space=pl.ANY)] * len(after),
        out_specs=pl.BlockSpec((ways, None, depth, rows, lanes), lambda k, g: (0, k, g, 0, 0)),
        out_shape=hbm(ways, count, channels, rows, lanes),
        scratch_shapes=[pltpu.VMEM((depth * rows * ways, lanes), jnp.float32)],
        compiler_params=pltpu.CompilerParams(vmem_limit_bytes=VMEM_BYTES),
        cost_estimate=cost(kernel_name, 0),
        name="pack_columns",
    )(*in_hbm([field, *after]))


def side_kernel(ways, me_ref, *refs):
    for x_ref, out_ref in zip(refs[:ways], refs[-ways:]):
        out_ref[...] = x_ref[...]


def rows_first(field, ways, me, after):
    channels, rows, cols, lanes = field.shape
    across = rows // ways

    def rows_of(step):
        return pl.BlockSpec(
            (channels, None, cols, lanes), lambda r, me: (0, (me[1] ^ step) * across + r, 0, 0)
        )

    return pl.pallas_call(
        functools.partial(side_kernel, ways),
        grid_spec=pltpu.PrefetchScalarGridSpec(
            num_scalar_prefetch=1,
            grid=(across,),
            in_specs=[rows_of(step) for step in range(ways)]
            + [pl.BlockSpec(memory_space=pl.ANY)],
            out_specs=[
                pl.BlockSpec((None, channels, cols, lanes), lambda r, me: (r, 0, 0, 0))
            ]
            * ways,
        ),
        out_shape=[hbm(across, channels, cols, lanes)] * ways,
        compiler_params=pltpu.CompilerParams(vmem_limit_bytes=VMEM_BYTES),
        cost_estimate=cost("rows", 0),
        name="rows_first",
    )(me, *in_hbm([field] * ways + [after]))


def mix_modes(mix_ref, spectra, mixed):
    mode_count, depth, _ = mix_ref.shape
    channels = depth // 2

    def one(mode, _):
        block = spectra[pl.ds(pl.multiple_of(mode * depth, depth), depth), :].astype(jnp.bfloat16)
        result = mm(mix_ref[mode], block)
        for part in range(2):
            mixed[pl.ds(part * mode_count + mode, channels, stride=2 * mode_count), :] = result[
                part * channels : (part + 1) * channels
            ]
        return 0

    lax.fori_loop(0, mode_count, one, 0, unroll=4)


def keep_spectra(spectra, result, channel, mode_count, channels, lanes):
    for at in range(2):
        for part in range(2):
            spectra[pl.ds(part * channels + channel + at, mode_count, stride=2 * channels), :] = (
                result[part * mode_count : (part + 1) * mode_count, at * lanes : (at + 1) * lanes]
            )


def mixed_pair(mixed, channel, coefs):
    start = pl.multiple_of(channel * coefs, 2 * coefs)
    return jnp.concatenate(
        [mixed[pl.ds(start, coefs), :], mixed[pl.ds(start + coefs, coefs), :]], axis=1
    ).astype(jnp.bfloat16)


def lines_kernel(ways, ft_ref, it_ref, mix_ref, *refs):
    refs, (spectra, mixed, wide) = refs[:-3], refs[-3:]
    count = len(refs) // 2
    pieces, outs = refs[:count], refs[count:]
    if count < ways:
        pieces = [pieces[0].at[way] for way in range(ways)]
        outs = [outs[0].at[way] for way in range(ways)]
    channels, length, lanes = pieces[0].shape
    mode_count = mix_ref.shape[0]
    total = ways * length

    def forward(pair, _):
        channel = 2 * pair
        right = jnp.concatenate(
            [stack_rows([piece[channel + at] for piece in pieces]) for at in range(2)], axis=1
        )
        keep_spectra(spectra, mm(ft_ref[...], right), channel, mode_count, channels, lanes)
        return 0

    lax.fori_loop(0, channels // 2, forward, 0, unroll=4)
    mix_modes(mix_ref, spectra, mixed)

    def inverse(pair, _):
        channel = 2 * pair
        result = mm(it_ref[...], mixed_pair(mixed, channel, 2 * mode_count))
        for at in range(2):
            wide[pl.ds(channel + at, total, stride=channels), :] = result[
                :, at * lanes : (at + 1) * lanes
            ]
        return 0

    lax.fori_loop(0, channels // 2, inverse, 0, unroll=4)
    for step in range(ways):
        part = wide[pl.ds(step * length * channels, length * channels), :]
        outs[step][...] = part.reshape(length, channels, lanes).astype(jnp.bfloat16)


def along_lines(kernel_name, pieces, weights, me, begin, count, after, done=None, held=()):
    stacked = not isinstance(pieces, list)
    if stacked:
        ways, several, channels, length, lanes = pieces.shape
        pieces = [pieces]
    else:
        ways = len(pieces)
        several, channels, length, lanes = pieces[0].shape
    mode_count = weights.shape[0]
    total = ways * length
    forward = forward_rows(total, mode_count)
    back = inverse_rows(total, mode_count).T
    if stacked:
        in_spec = pl.BlockSpec(
            (ways, None, channels, length, lanes), lambda g: (0, begin + g, 0, 0, 0)
        )
        out_spec = pl.BlockSpec((ways, None, length, channels, lanes), lambda g: (0, g, 0, 0, 0))
        out_shape = hbm(ways, count, length, channels, lanes)
    else:
        order = me ^ jnp.arange(ways)
        forward = forward.reshape(2 * mode_count, ways, length)
        forward = jnp.take(forward, order, axis=1).reshape(2 * mode_count, total)
        back = back.reshape(ways, length, 2 * mode_count)
        back = jnp.take(back, order, axis=0).reshape(total, 2 * mode_count)
        in_spec = pl.BlockSpec((None, channels, length, lanes), lambda g: (begin + g, 0, 0, 0))
        out_spec = pl.BlockSpec((None, length, channels, lanes), lambda g: (begin + g, 0, 0, 0))
        out_shape = hbm(several, length, channels, lanes)
    whole = lambda shape: pl.BlockSpec(shape, lambda g: (0,) * len(shape))
    kept = list(done or ()) + list(held)
    moved = 0 if done else len(pieces)
    idle = kept + list(after)
    last = len(idle) + 3 + 2 * len(pieces)
    elsewhere = pl.BlockSpec(memory_space=pl.ANY)
    return pl.pallas_call(
        lambda *refs: lines_kernel(ways, *refs[len(idle) : last], *refs[-3:]),
        grid=(count,),
        in_specs=[elsewhere] * len(idle)
        + [whole(forward.shape), whole(back.shape), whole(weights.shape)]
        + [in_spec] * len(pieces),
        out_specs=[out_spec] * len(pieces) + [elsewhere] * len(held),
        out_shape=[out_shape] * len(pieces) + [hbm(*array.shape) for array in held],
        input_output_aliases={at: moved + at for at in range(len(kept))},
        scratch_shapes=[
            pltpu.VMEM((2 * channels * mode_count, lanes), jnp.float32),
            pltpu.VMEM((2 * channels * mode_count, lanes), jnp.float32),
            pltpu.VMEM((total * channels, lanes), jnp.float32),
        ],
        compiler_params=pltpu.CompilerParams(vmem_limit_bytes=VMEM_BYTES),
        cost_estimate=cost(kernel_name, 0),
        name="line_branch",
    )(*in_hbm(idle), forward, back, *in_hbm([weights, *pieces]))


def last_kernel(ft_ref, it_ref, mix_ref, x_ref, out_ref, spectra, mixed, wide):
    channels, rows, cols, length = x_ref.shape
    mode_count = mix_ref.shape[0]
    cells = rows * cols

    def forward(pair, _):
        channel = 2 * pair
        right = jnp.concatenate(
            [x_ref[channel + at].reshape(cells, length) for at in range(2)], axis=0
        )
        keep_spectra(
            spectra, mm(ft_ref[...], right, (1, 1)), channel, mode_count, channels, cells
        )
        return 0

    lax.fori_loop(0, channels // 2, forward, 0, unroll=4)
    mix_modes(mix_ref, spectra, mixed)

    def inverse(pair, _):
        channel = 2 * pair
        result = mm(mixed_pair(mixed, channel, 2 * mode_count), it_ref[...], (0, 0))
        for at in range(2):
            wide[pl.ds(channel + at, cells, stride=channels), :] = result[
                at * cells : (at + 1) * cells
            ]
        return 0

    lax.fori_loop(0, channels // 2, inverse, 0, unroll=4)
    out_ref[...] = wide[...].reshape(rows, cols, channels, length).astype(jnp.bfloat16)


def last_branch(kernel_name, field, weights, part, parts, done, after, held=()):
    channels, rows, cols, length = field.shape
    mode_count = weights.shape[0]
    block = max(1, min(rows // parts, 128 // cols))
    steps = rows // block // parts
    forward, back = forward_rows(length, mode_count), inverse_rows(length, mode_count)
    whole = lambda shape: pl.BlockSpec(shape, lambda g: (0,) * len(shape))
    elsewhere = pl.BlockSpec(memory_space=pl.ANY)
    kept = ([] if done is None else [done]) + list(held)
    moved = 1 if done is None else 0
    idle = kept + list(after)
    return pl.pallas_call(
        lambda *refs: last_kernel(*refs[len(idle) : len(idle) + 5], *refs[-3:]),
        grid=(steps,),
        in_specs=[elsewhere] * len(idle)
        + [
            whole(forward.shape),
            whole(back.shape),
            whole(weights.shape),
            pl.BlockSpec(
                (channels, block, cols, length), lambda g: (0, part * steps + g, 0, 0)
            ),
        ],
        out_specs=[
            pl.BlockSpec((block, cols, channels, length), lambda g: (part * steps + g, 0, 0, 0))
        ]
        + [elsewhere] * len(held),
        out_shape=[hbm(rows, cols, channels, length)] + [hbm(*array.shape) for array in held],
        input_output_aliases={at: moved + at for at in range(len(kept))},
        scratch_shapes=[
            pltpu.VMEM((2 * channels * mode_count, block * cols), jnp.float32),
            pltpu.VMEM((2 * channels * mode_count, block * cols), jnp.float32),
            pltpu.VMEM((block * cols * channels, length), jnp.float32),
        ],
        compiler_params=pltpu.CompilerParams(vmem_limit_bytes=VMEM_BYTES),
        cost_estimate=cost(kernel_name, 0),
        name="last_branch",
    )(*in_hbm(idle), forward, back, *in_hbm([weights, field]))


def cell_kernel(col_ways, me_ref, x_ref, win_ref, wout_ref, bin_ref, bout_ref, *refs):
    first_ref, second, third_ref = refs[0], refs[1 : 1 + col_ways], refs[1 + col_ways]
    out_ref, now, wide = refs[-3:]
    channels, _, ways, lanes = x_ref.shape

    for step in range(col_ways):

        @pl.when(pl.program_id(0) == step)
        def _():
            now[...] = second[step][...]

    for col in range(0, ways, 2):
        summed = []
        for at in range(2):
            pair = first_ref[col + at].astype(jnp.float32) + now[col + at].astype(jnp.float32)
            pair = pair.astype(jnp.bfloat16).astype(jnp.float32)
            total = pair + third_ref[col + at].astype(jnp.float32)
            summed.append(total.astype(jnp.bfloat16))
        pre = mm(win_ref[...], jnp.concatenate(summed, axis=1)) + bin_ref[...]
        hidden = (0.5 * pre * (1.0 + lax.erf(pre * HALF_ROOT))).astype(jnp.bfloat16)
        result = mm(wout_ref[...], hidden) + bout_ref[...]
        for at in range(2):
            wide[pl.ds(col + at, channels, stride=ways), :] = result[
                :, at * lanes : (at + 1) * lanes
            ]
    total = wide[...].reshape(channels, ways, lanes) + x_ref[:, 0].astype(jnp.float32)
    out_ref[:, 0] = total.astype(jnp.bfloat16)


def cells(field, first, which, second, third, ffn, chunk, me, done, after):
    channels, rows, cols, lanes = field.shape
    ways, col_ways = first.shape[0], len(second)
    across = rows // col_ways

    def row(step, at, me):
        return (me[1] ^ step) * across + at

    def own_row(which):
        def index(step, at, me):
            now = jnp.where(step == which, at, jnp.where(step < which, 0, across - 1))
            return now, chunk, 0, 0

        return pl.BlockSpec((None, ways, channels, lanes), index)

    whole = lambda shape: pl.BlockSpec(shape, lambda *_: (0,) * len(shape))
    tile = pl.BlockSpec((channels, 1, ways, lanes), lambda s, a, me: (0, row(s, a, me), chunk, 0))
    in_specs = [tile] + [whole(w.shape) for w in ffn]
    in_specs.append(
        pl.BlockSpec(
            (ways, None, None, channels, lanes),
            lambda s, a, me: (0, which, row(s, a, me), 0, 0),
        )
    )
    in_specs += [own_row(step) for step in range(col_ways)]
    in_specs.append(
        pl.BlockSpec((None, ways, channels, lanes), lambda s, a, me: (row(s, a, me), chunk, 0, 0))
    )
    operands = [me, *in_hbm([field]), *ffn, *in_hbm([first, *second, third])]
    aliases = {}
    if done is not None:
        aliases = {len(operands): 0}
    for array in (done, after):
        if array is not None:
            in_specs.append(pl.BlockSpec(memory_space=pl.ANY))
            operands += in_hbm([array])
    return pl.pallas_call(
        functools.partial(cell_kernel, col_ways),
        grid_spec=pltpu.PrefetchScalarGridSpec(
            num_scalar_prefetch=1,
            grid=(col_ways, across),
            in_specs=in_specs,
            out_specs=tile,
            scratch_shapes=[
                pltpu.VMEM((ways, channels, lanes), jnp.bfloat16),
                pltpu.VMEM((channels * ways, lanes), jnp.float32),
            ],
        ),
        out_shape=hbm(*field.shape),
        input_output_aliases=aliases,
        compiler_params=pltpu.CompilerParams(vmem_limit_bytes=VMEM_BYTES),
        cost_estimate=cost(f"ffn{chunk}", 0),
        name="feed_forward",
    )(*operands)


def swap(piece, axis, step):
    ways = lax.axis_size(axis)
    return lax.ppermute(piece, axis, [(at, at ^ step) for at in range(ways)])


def exchange(pieces, axis, skip=None):
    return [
        swap(piece, axis, step) if step not in (0, skip) else piece
        for step, piece in enumerate(pieces)
    ]


def trade(stack):
    return lax.all_to_all(stack, "row", split_axis=0, concat_axis=0)


def body(field, spec_first, spec_second, spec_third, ffn_in, ffn_out, bias_in, bias_out):
    channels, rows, cols, lanes = field.shape
    ways, col_ways = lax.axis_size("row"), lax.axis_size("col")
    row_me, col_me = lax.axis_index("row"), lax.axis_index("col")
    me = jnp.stack([row_me, col_me]).astype(jnp.int32)
    chunks = cols // ways
    across = rows // col_ways
    ffn = (ffn_in.T, ffn_out.T, bias_in[:, None], bias_out[:, None])

    early_count = max(1, min(PLAN["early"], chunks - 1))
    rest = chunks - early_count
    seen = {}

    def pins(kernel):
        return [seen[name][place] for name, place in PLAN["pins"].get(kernel, ())]

    early = pack("pack0", field, 0, early_count, ways, [])
    early_in = trade(early)
    late = pack("pack1", field, early_count, rest, ways, [early])
    late_in = trade(late)
    seen["early"], seen["late"] = [early_in], [late_in]
    corner = 3
    side = list(rows_first(field, col_ways, me, early))
    seen["side"] = side_in = exchange(side, "col", skip=corner)
    first_mix, second_mix, third_mix = mix_rows(side[0], spec_first, spec_second, spec_third)

    def last(part, done, after):
        name = f"last{part}"
        held = [side[corner]] if PLAN["corner"] == name else []
        got = last_branch(name, field, third_mix, part, 2, done, after + pins(name), held)
        if held:
            side[corner] = got[1]
        return got[0]

    third = last(0, None, [])
    if PLAN["last"] == 0:
        third = last(1, third, [])
    side_in[corner] = swap(side[corner], "col", corner)
    parts = along_lines(
        "dim1", early_in, first_mix, None, 0, early_count, [third] + pins("dim1")
    )[0]
    token = parts
    if PLAN["last"] == 1:
        third = last(1, third, [token])
        token = third
    cut = across // 2
    second = along_lines(
        "dim2a", side_in, second_mix, col_me, 0, cut, [token] + pins("dim2a")
    )
    token = second[0]
    if PLAN["last"] == 2:
        third = last(1, third, [token])
        token = third
    second = along_lines(
        "dim2b",
        side_in,
        second_mix,
        col_me,
        cut,
        across - cut,
        [token] + pins("dim2b"),
        done=second,
        held=[parts],
    )
    second, parts = second[:-1], second[-1]
    back = [(trade(parts), early_count)]
    token = second[0]
    second_in = exchange(second, "col")
    seen["second"] = second_in
    if PLAN["last"] == 3:
        third = last(1, third, [token])
        token = third
    groups = PLAN["groups"] if sum(PLAN["groups"]) == rest else [1] * rest
    begin = 0
    for at, count in enumerate(groups):
        name = f"late{at}"
        parts = along_lines(name, late_in, first_mix, None, begin, count, [token] + pins(name))[0]
        back.append((trade(parts), count))
        begin += count
        token = parts
    if PLAN["last"] == 4:
        third = last(1, third, [token])
        token = third

    result, chunk = None, 0
    for branch, count in back:
        for which in range(count):
            result = cells(
                field, branch, which, second_in, third, ffn, chunk, me, result, token
            )
            chunk, token = chunk + 1, None
    return result


def solution(mesh):
    return jax.shard_map(
        body,
        mesh=mesh,
        in_specs=(P("grp", "row", "col", None), P(), P(), P(), P(), P(), P(), P()),
        out_specs=P("grp", "row", "col", None),
        check_vma=False,
    )
```

```python
import functools
import math

import jax
import jax.numpy as jnp
from jax import lax
from jax.experimental import pallas as pl
from jax.experimental.pallas import tpu as pltpu
from jax.sharding import PartitionSpec as P

MIB = 1024 * 1024
VMEM_BYTES = 62 * MIB
PLAN = {
    "early": 2,
    "groups": [1, 1],
    "last": 0,
    "corner": "",
    "pins": {"late0": [("second", 1), ("second", 2), ("second", 3)]},
    "cost": {"pack0": 8.0, "pack1": 8.0, "rows": 7.6, "mix": 5.0, "last0": 22.0, "last1": 22.0, "dim1": 20.0, "dim2a": 20.0, "dim2b": 20.0, "late0": 200.0, "late1": 10.0, "ffn0": 21.0, "ffn1": 21.0, "ffn2": 21.0, "ffn3": 21.0},
}
HALF_ROOT = math.sqrt(0.5)


def forward_rows(length, mode_count):
    grid_pos = jnp.arange(length, dtype=jnp.int32)[None, :]
    mode_location = jnp.arange(mode_count, dtype=jnp.int32)[:, None]
    phase = (grid_pos * mode_location % length).astype(jnp.float32) * (2.0 * math.pi / length)
    return jnp.concatenate([jnp.cos(phase), -jnp.sin(phase)], axis=0).astype(jnp.bfloat16)


def inverse_rows(length, mode_count):
    mode_location = jnp.arange(mode_count, dtype=jnp.int32)[:, None]
    grid_pos = jnp.arange(length, dtype=jnp.int32)[None, :]
    phase = (grid_pos * mode_location % length).astype(jnp.float32) * (2.0 * math.pi / length)
    factor = jnp.where(mode_location == 0, 1.0, 2.0).astype(jnp.float32) / length
    return jnp.concatenate(
        [factor * jnp.cos(phase), -factor * jnp.sin(phase)], axis=0
    ).astype(jnp.bfloat16)


def mix_kernel(*refs):
    count = len(refs) // 2
    for spec, out in zip(refs[:count], refs[count:]):
        channels = spec.shape[-1]
        for mode in range(spec.shape[1]):
            real = spec[0, mode].astype(jnp.float32).T
            imag = spec[1, mode].astype(jnp.float32).T
            upper = jnp.concatenate([real, -imag], axis=1)
            lower = jnp.concatenate([imag, real], axis=1)
            out[mode, :channels] = upper.astype(jnp.bfloat16)
            out[mode, channels:] = lower.astype(jnp.bfloat16)


def mix_rows(after, *specs):
    _, mode_count, channels, _ = specs[0].shape
    block = min(8, mode_count)
    kernel, token_specs, token = ordered(mix_kernel, after)
    return pl.pallas_call(
        kernel,
        grid=(mode_count // block,),
        in_specs=token_specs
        + [pl.BlockSpec((2, block, channels, channels), lambda g: (0, g, 0, 0))]
        * len(specs),
        out_specs=[pl.BlockSpec((block, 2 * channels, 2 * channels), lambda g: (g, 0, 0))]
        * len(specs),
        out_shape=[hbm(mode_count, 2 * channels, 2 * channels)] * len(specs),
        compiler_params=pltpu.CompilerParams(vmem_limit_bytes=VMEM_BYTES),
        cost_estimate=cost("mix", 0),
        name="mixing_matrices",
    )(*token, *in_hbm(specs))


def hbm(*shape):
    return pltpu.HBM(shape, jnp.bfloat16)


def in_hbm(arrays):
    return [pltpu.with_memory_space_constraint(array, pltpu.HBM) for array in arrays]


def cost(kernel, size):
    micros = PLAN["cost"].get(kernel, 3.0)
    return pl.CostEstimate(
        flops=int(micros * 1.15e9), bytes_accessed=int(size), transcendentals=0
    )


def ordered(kernel, after):
    if after is None:
        return kernel, [], []
    return (
        lambda _, *refs: kernel(*refs),
        [pl.BlockSpec(memory_space=pl.ANY)],
        in_hbm([after]),
    )


def mm(left, right, dims=(1, 0)):
    return lax.dot_general(
        left, right, (((dims[0],), (dims[1],)), ((), ())), preferred_element_type=jnp.float32
    )


def stack_rows(parts):
    if parts[0].shape[0] % 16 == 0:
        return jnp.concatenate(parts, axis=0)
    return jnp.concatenate([p.astype(jnp.float32) for p in parts], axis=0).astype(jnp.bfloat16)


def pack_kernel(x_ref, *refs):
    out_ref, wide = refs[-2:]
    channels, rows, ways, lanes = x_ref.shape
    wide[...] = x_ref[...].astype(jnp.float32).reshape(channels * rows * ways, lanes)
    for way in range(ways):
        picked = wide[pl.ds(way, channels * rows, stride=ways), :]
        out_ref[way] = picked.reshape(channels, rows, lanes).astype(jnp.bfloat16)


def pack(kernel_name, field, first, count, ways, after):
    channels, rows, _, lanes = field.shape
    depth = min(16, channels)
    return pl.pallas_call(
        pack_kernel,
        grid=(count, channels // depth),
        in_specs=[pl.BlockSpec((depth, rows, ways, lanes), lambda k, g: (g, 0, first + k, 0))]
        + [pl.BlockSpec(memory_space=pl.ANY)] * len(after),
        out_specs=pl.BlockSpec((ways, None, depth, rows, lanes), lambda k, g: (0, k, g, 0, 0)),
        out_shape=hbm(ways, count, channels, rows, lanes),
        scratch_shapes=[pltpu.VMEM((depth * rows * ways, lanes), jnp.float32)],
        compiler_params=pltpu.CompilerParams(vmem_limit_bytes=VMEM_BYTES),
        cost_estimate=cost(kernel_name, 0),
        name="pack_columns",
    )(*in_hbm([field, *after]))


def side_kernel(ways, me_ref, *refs):
    for x_ref, out_ref in zip(refs[:ways], refs[-ways:]):
        out_ref[...] = x_ref[...]


def rows_first(field, ways, me, after):
    channels, rows, cols, lanes = field.shape
    across = rows // ways

    def rows_of(step):
        return pl.BlockSpec(
            (channels, None, cols, lanes), lambda r, me: (0, (me[1] ^ step) * across + r, 0, 0)
        )

    return pl.pallas_call(
        functools.partial(side_kernel, ways),
        grid_spec=pltpu.PrefetchScalarGridSpec(
            num_scalar_prefetch=1,
            grid=(across,),
            in_specs=[rows_of(step) for step in range(ways)]
            + [pl.BlockSpec(memory_space=pl.ANY)],
            out_specs=[
                pl.BlockSpec((None, channels, cols, lanes), lambda r, me: (r, 0, 0, 0))
            ]
            * ways,
        ),
        out_shape=[hbm(across, channels, cols, lanes)] * ways,
        compiler_params=pltpu.CompilerParams(vmem_limit_bytes=VMEM_BYTES),
        cost_estimate=cost("rows", 0),
        name="rows_first",
    )(me, *in_hbm([field] * ways + [after]))


def mix_modes(mix_ref, spectra, mixed):
    mode_count, depth, _ = mix_ref.shape
    channels = depth // 2

    def one(mode, _):
        block = spectra[pl.ds(pl.multiple_of(mode * depth, depth), depth), :].astype(jnp.bfloat16)
        result = mm(mix_ref[mode], block)
        for part in range(2):
            mixed[pl.ds(part * mode_count + mode, channels, stride=2 * mode_count), :] = result[
                part * channels : (part + 1) * channels
            ]
        return 0

    lax.fori_loop(0, mode_count, one, 0, unroll=4)


def keep_spectra(spectra, result, channel, mode_count, channels, lanes):
    for at in range(2):
        for part in range(2):
            spectra[pl.ds(part * channels + channel + at, mode_count, stride=2 * channels), :] = (
                result[part * mode_count : (part + 1) * mode_count, at * lanes : (at + 1) * lanes]
            )


def mixed_pair(mixed, channel, coefs):
    start = pl.multiple_of(channel * coefs, 2 * coefs)
    return jnp.concatenate(
        [mixed[pl.ds(start, coefs), :], mixed[pl.ds(start + coefs, coefs), :]], axis=1
    ).astype(jnp.bfloat16)


def lines_kernel(ways, ft_ref, it_ref, mix_ref, *refs):
    refs, (spectra, mixed, wide) = refs[:-3], refs[-3:]
    count = len(refs) // 2
    pieces, outs = refs[:count], refs[count:]
    if count < ways:
        pieces = [pieces[0].at[way] for way in range(ways)]
        outs = [outs[0].at[way] for way in range(ways)]
    channels, length, lanes = pieces[0].shape
    mode_count = mix_ref.shape[0]
    total = ways * length

    def forward(pair, _):
        channel = 2 * pair
        right = jnp.concatenate(
            [stack_rows([piece[channel + at] for piece in pieces]) for at in range(2)], axis=1
        )
        keep_spectra(spectra, mm(ft_ref[...], right), channel, mode_count, channels, lanes)
        return 0

    lax.fori_loop(0, channels // 2, forward, 0, unroll=4)
    mix_modes(mix_ref, spectra, mixed)

    def inverse(pair, _):
        channel = 2 * pair
        result = mm(it_ref[...], mixed_pair(mixed, channel, 2 * mode_count))
        for at in range(2):
            wide[pl.ds(channel + at, total, stride=channels), :] = result[
                :, at * lanes : (at + 1) * lanes
            ]
        return 0

    lax.fori_loop(0, channels // 2, inverse, 0, unroll=4)
    for step in range(ways):
        part = wide[pl.ds(step * length * channels, length * channels), :]
        outs[step][...] = part.reshape(length, channels, lanes).astype(jnp.bfloat16)


def along_lines(kernel_name, pieces, weights, me, begin, count, after, done=None, held=()):
    stacked = not isinstance(pieces, list)
    if stacked:
        ways, several, channels, length, lanes = pieces.shape
        pieces = [pieces]
    else:
        ways = len(pieces)
        several, channels, length, lanes = pieces[0].shape
    mode_count = weights.shape[0]
    total = ways * length
    forward = forward_rows(total, mode_count)
    back = inverse_rows(total, mode_count).T
    if stacked:
        in_spec = pl.BlockSpec(
            (ways, None, channels, length, lanes), lambda g: (0, begin + g, 0, 0, 0)
        )
        out_spec = pl.BlockSpec((ways, None, length, channels, lanes), lambda g: (0, g, 0, 0, 0))
        out_shape = hbm(ways, count, length, channels, lanes)
    else:
        order = me ^ jnp.arange(ways)
        forward = forward.reshape(2 * mode_count, ways, length)
        forward = jnp.take(forward, order, axis=1).reshape(2 * mode_count, total)
        back = back.reshape(ways, length, 2 * mode_count)
        back = jnp.take(back, order, axis=0).reshape(total, 2 * mode_count)
        in_spec = pl.BlockSpec((None, channels, length, lanes), lambda g: (begin + g, 0, 0, 0))
        out_spec = pl.BlockSpec((None, length, channels, lanes), lambda g: (begin + g, 0, 0, 0))
        out_shape = hbm(several, length, channels, lanes)
    whole = lambda shape: pl.BlockSpec(shape, lambda g: (0,) * len(shape))
    kept = list(done or ()) + list(held)
    moved = 0 if done else len(pieces)
    idle = kept + list(after)
    last = len(idle) + 3 + 2 * len(pieces)
    elsewhere = pl.BlockSpec(memory_space=pl.ANY)
    return pl.pallas_call(
        lambda *refs: lines_kernel(ways, *refs[len(idle) : last], *refs[-3:]),
        grid=(count,),
        in_specs=[elsewhere] * len(idle)
        + [whole(forward.shape), whole(back.shape), whole(weights.shape)]
        + [in_spec] * len(pieces),
        out_specs=[out_spec] * len(pieces) + [elsewhere] * len(held),
        out_shape=[out_shape] * len(pieces) + [hbm(*array.shape) for array in held],
        input_output_aliases={at: moved + at for at in range(len(kept))},
        scratch_shapes=[
            pltpu.VMEM((2 * channels * mode_count, lanes), jnp.float32),
            pltpu.VMEM((2 * channels * mode_count, lanes), jnp.float32),
            pltpu.VMEM((total * channels, lanes), jnp.float32),
        ],
        compiler_params=pltpu.CompilerParams(vmem_limit_bytes=VMEM_BYTES),
        cost_estimate=cost(kernel_name, 0),
        name="line_branch",
    )(*in_hbm(idle), forward, back, *in_hbm([weights, *pieces]))


def last_kernel(ft_ref, it_ref, mix_ref, x_ref, out_ref, spectra, mixed, wide):
    channels, rows, cols, length = x_ref.shape
    mode_count = mix_ref.shape[0]
    cells = rows * cols

    def forward(pair, _):
        channel = 2 * pair
        right = jnp.concatenate(
            [x_ref[channel + at].reshape(cells, length) for at in range(2)], axis=0
        )
        keep_spectra(
            spectra, mm(ft_ref[...], right, (1, 1)), channel, mode_count, channels, cells
        )
        return 0

    lax.fori_loop(0, channels // 2, forward, 0, unroll=4)
    mix_modes(mix_ref, spectra, mixed)

    def inverse(pair, _):
        channel = 2 * pair
        result = mm(mixed_pair(mixed, channel, 2 * mode_count), it_ref[...], (0, 0))
        for at in range(2):
            wide[pl.ds(channel + at, cells, stride=channels), :] = result[
                at * cells : (at + 1) * cells
            ]
        return 0

    lax.fori_loop(0, channels // 2, inverse, 0, unroll=4)
    out_ref[...] = wide[...].reshape(rows, cols, channels, length).astype(jnp.bfloat16)


def last_branch(kernel_name, field, weights, part, parts, done, after, held=()):
    channels, rows, cols, length = field.shape
    mode_count = weights.shape[0]
    block = max(1, min(rows // parts, 128 // cols))
    steps = rows // block // parts
    forward, back = forward_rows(length, mode_count), inverse_rows(length, mode_count)
    whole = lambda shape: pl.BlockSpec(shape, lambda g: (0,) * len(shape))
    elsewhere = pl.BlockSpec(memory_space=pl.ANY)
    kept = ([] if done is None else [done]) + list(held)
    moved = 1 if done is None else 0
    idle = kept + list(after)
    return pl.pallas_call(
        lambda *refs: last_kernel(*refs[len(idle) : len(idle) + 5], *refs[-3:]),
        grid=(steps,),
        in_specs=[elsewhere] * len(idle)
        + [
            whole(forward.shape),
            whole(back.shape),
            whole(weights.shape),
            pl.BlockSpec(
                (channels, block, cols, length), lambda g: (0, part * steps + g, 0, 0)
            ),
        ],
        out_specs=[
            pl.BlockSpec((block, cols, channels, length), lambda g: (part * steps + g, 0, 0, 0))
        ]
        + [elsewhere] * len(held),
        out_shape=[hbm(rows, cols, channels, length)] + [hbm(*array.shape) for array in held],
        input_output_aliases={at: moved + at for at in range(len(kept))},
        scratch_shapes=[
            pltpu.VMEM((2 * channels * mode_count, block * cols), jnp.float32),
            pltpu.VMEM((2 * channels * mode_count, block * cols), jnp.float32),
            pltpu.VMEM((block * cols * channels, length), jnp.float32),
        ],
        compiler_params=pltpu.CompilerParams(vmem_limit_bytes=VMEM_BYTES),
        cost_estimate=cost(kernel_name, 0),
        name="last_branch",
    )(*in_hbm(idle), forward, back, *in_hbm([weights, field]))


def cell_kernel(col_ways, me_ref, x_ref, win_ref, wout_ref, bin_ref, bout_ref, *refs):
    first_ref, second, third_ref = refs[0], refs[1 : 1 + col_ways], refs[1 + col_ways]
    out_ref, now, wide = refs[-3:]
    channels, _, ways, lanes = x_ref.shape

    for step in range(col_ways):

        @pl.when(pl.program_id(0) == step)
        def _():
            now[...] = second[step][...]

    for col in range(0, ways, 2):
        summed = []
        for at in range(2):
            pair = first_ref[col + at].astype(jnp.float32) + now[col + at].astype(jnp.float32)
            pair = pair.astype(jnp.bfloat16).astype(jnp.float32)
            total = pair + third_ref[col + at].astype(jnp.float32)
            summed.append(total.astype(jnp.bfloat16))
        pre = mm(win_ref[...], jnp.concatenate(summed, axis=1)) + bin_ref[...]
        hidden = (0.5 * pre * (1.0 + lax.erf(pre * HALF_ROOT))).astype(jnp.bfloat16)
        result = mm(wout_ref[...], hidden) + bout_ref[...]
        for at in range(2):
            wide[pl.ds(col + at, channels, stride=ways), :] = result[
                :, at * lanes : (at + 1) * lanes
            ]
    total = wide[...].reshape(channels, ways, lanes) + x_ref[:, 0].astype(jnp.float32)
    out_ref[:, 0] = total.astype(jnp.bfloat16)


def cells(field, first, which, second, third, ffn, chunk, me, done, after):
    channels, rows, cols, lanes = field.shape
    ways, col_ways = first.shape[0], len(second)
    across = rows // col_ways

    def row(step, at, me):
        return (me[1] ^ step) * across + at

    def own_row(which):
        def index(step, at, me):
            now = jnp.where(step == which, at, jnp.where(step < which, 0, across - 1))
            return now, chunk, 0, 0

        return pl.BlockSpec((None, ways, channels, lanes), index)

    whole = lambda shape: pl.BlockSpec(shape, lambda *_: (0,) * len(shape))
    tile = pl.BlockSpec((channels, 1, ways, lanes), lambda s, a, me: (0, row(s, a, me), chunk, 0))
    in_specs = [tile] + [whole(w.shape) for w in ffn]
    in_specs.append(
        pl.BlockSpec(
            (ways, None, None, channels, lanes),
            lambda s, a, me: (0, which, row(s, a, me), 0, 0),
        )
    )
    in_specs += [own_row(step) for step in range(col_ways)]
    in_specs.append(
        pl.BlockSpec((None, ways, channels, lanes), lambda s, a, me: (row(s, a, me), chunk, 0, 0))
    )
    operands = [me, *in_hbm([field]), *ffn, *in_hbm([first, *second, third])]
    aliases = {}
    if done is not None:
        aliases = {len(operands): 0}
    for array in (done, after):
        if array is not None:
            in_specs.append(pl.BlockSpec(memory_space=pl.ANY))
            operands += in_hbm([array])
    return pl.pallas_call(
        functools.partial(cell_kernel, col_ways),
        grid_spec=pltpu.PrefetchScalarGridSpec(
            num_scalar_prefetch=1,
            grid=(col_ways, across),
            in_specs=in_specs,
            out_specs=tile,
            scratch_shapes=[
                pltpu.VMEM((ways, channels, lanes), jnp.bfloat16),
                pltpu.VMEM((channels * ways, lanes), jnp.float32),
            ],
        ),
        out_shape=hbm(*field.shape),
        input_output_aliases=aliases,
        compiler_params=pltpu.CompilerParams(vmem_limit_bytes=VMEM_BYTES),
        cost_estimate=cost(f"ffn{chunk}", 0),
        name="feed_forward",
    )(*operands)


def swap(piece, axis, step):
    ways = lax.axis_size(axis)
    return lax.ppermute(piece, axis, [(at, at ^ step) for at in range(ways)])


def exchange(pieces, axis, skip=None):
    return [
        swap(piece, axis, step) if step not in (0, skip) else piece
        for step, piece in enumerate(pieces)
    ]


def trade(stack):
    return lax.all_to_all(stack, "row", split_axis=0, concat_axis=0)


def body(field, spec_first, spec_second, spec_third, ffn_in, ffn_out, bias_in, bias_out):
    channels, rows, cols, lanes = field.shape
    ways, col_ways = lax.axis_size("row"), lax.axis_size("col")
    row_me, col_me = lax.axis_index("row"), lax.axis_index("col")
    me = jnp.stack([row_me, col_me]).astype(jnp.int32)
    chunks = cols // ways
    across = rows // col_ways
    ffn = (ffn_in.T, ffn_out.T, bias_in[:, None], bias_out[:, None])

    early_count = max(1, min(PLAN["early"], chunks - 1))
    rest = chunks - early_count
    seen = {}

    def pins(kernel):
        return [seen[name][place] for name, place in PLAN["pins"].get(kernel, ())]

    early = pack("pack0", field, 0, early_count, ways, [])
    early_in = trade(early)
    corner = 3
    side = list(rows_first(field, col_ways, me, early))
    seen["side"] = side_in = exchange(side, "col", skip=corner)
    first_mix, second_mix, third_mix = mix_rows(side[0], spec_first, spec_second, spec_third)

    def last(part, done, after):
        name = f"last{part}"
        held = [side[corner]] if PLAN["corner"] == name else []
        got = last_branch(name, field, third_mix, part, 2, done, after + pins(name), held)
        if held:
            side[corner] = got[1]
        return got[0]

    third = last(0, None, [])
    if PLAN["last"] == 0:
        third = last(1, third, [])
    late_in = trade(pack("pack1", field, early_count, rest, ways, [third]))
    side_in[corner] = swap(side[corner], "col", corner)
    parts = along_lines(
        "dim1", early_in, first_mix, None, 0, early_count, [third] + pins("dim1")
    )[0]
    token = parts
    if PLAN["last"] == 1:
        third = last(1, third, [token])
        token = third
    cut = across // 2
    second = along_lines(
        "dim2a", side_in, second_mix, col_me, 0, cut, [token] + pins("dim2a")
    )
    token = second[0]
    if PLAN["last"] == 2:
        third = last(1, third, [token])
        token = third
    second = along_lines(
        "dim2b",
        side_in,
        second_mix,
        col_me,
        cut,
        across - cut,
        [token] + pins("dim2b"),
        done=second,
        held=[parts],
    )
    second, parts = second[:-1], second[-1]
    back = [(trade(parts), early_count)]
    token = second[0]
    second_in = exchange(second, "col")
    seen["second"] = second_in
    if PLAN["last"] == 3:
        third = last(1, third, [token])
        token = third
    groups = PLAN["groups"] if sum(PLAN["groups"]) == rest else [1] * rest
    begin = 0
    ready = []
    for at, count in enumerate(groups):
        name = f"late{at}"
        parts, *ready = along_lines(
            name, late_in, first_mix, None, begin, count, [token] + pins(name), held=ready
        )
        ready.append(parts)
        begin += count
        token = parts
    back += [(trade(parts), count) for parts, count in zip(ready, groups)]
    if PLAN["last"] == 4:
        third = last(1, third, [token])
        token = third

    result, chunk = None, 0
    for branch, count in back:
        for which in range(count):
            result = cells(
                field, branch, which, second_in, third, ffn, chunk, me, result, token
            )
            chunk, token = chunk + 1, None
    return result


def solution(mesh):
    return jax.shard_map(
        body,
        mesh=mesh,
        in_specs=(P("grp", "row", "col", None), P(), P(), P(), P(), P(), P(), P()),
        out_specs=P("grp", "row", "col", None),
        check_vma=False,
    )
```

```python
import functools
import math

import jax
import jax.numpy as jnp
from jax import lax
from jax.experimental import pallas as pl
from jax.experimental.pallas import tpu as pltpu
from jax.sharding import PartitionSpec as P

MIB = 1024 * 1024
VMEM_BYTES = 62 * MIB
COSTS = {
    "pack0": 8.0,
    "pack1": 8.0,
    "rows": 7.6,
    "mix": 5.0,
    "last0": 22.0,
    "last1": 22.0,
    "dim1": 20.0,
    "dim2a": 20.0,
    "dim2b": 20.0,
    "late0": 200.0,
    "late1": 10.0,
    "ffn0": 2.0,
    "ffn1": 2.0,
    "ffn2": 60.0,
    "ffn3": 60.0,
    "ffn4": 11.0,
}
HALF_ROOT = math.sqrt(0.5)


def forward_rows(length, mode_count):
    grid_pos = jnp.arange(length, dtype=jnp.int32)[None, :]
    mode_location = jnp.arange(mode_count, dtype=jnp.int32)[:, None]
    phase = (grid_pos * mode_location % length).astype(jnp.float32) * (2.0 * math.pi / length)
    return jnp.concatenate([jnp.cos(phase), -jnp.sin(phase)], axis=0).astype(jnp.bfloat16)


def inverse_rows(length, mode_count):
    mode_location = jnp.arange(mode_count, dtype=jnp.int32)[:, None]
    grid_pos = jnp.arange(length, dtype=jnp.int32)[None, :]
    phase = (grid_pos * mode_location % length).astype(jnp.float32) * (2.0 * math.pi / length)
    factor = jnp.where(mode_location == 0, 1.0, 2.0).astype(jnp.float32) / length
    return jnp.concatenate(
        [factor * jnp.cos(phase), -factor * jnp.sin(phase)], axis=0
    ).astype(jnp.bfloat16)


def mix_kernel(*refs):
    count = len(refs) // 2
    for spec, out in zip(refs[:count], refs[count:]):
        channels = spec.shape[-1]
        for mode in range(spec.shape[1]):
            real = spec[0, mode].astype(jnp.float32).T
            imag = spec[1, mode].astype(jnp.float32).T
            upper = jnp.concatenate([real, -imag], axis=1)
            lower = jnp.concatenate([imag, real], axis=1)
            out[mode, :channels] = upper.astype(jnp.bfloat16)
            out[mode, channels:] = lower.astype(jnp.bfloat16)


def mix_rows(after, *specs):
    _, mode_count, channels, _ = specs[0].shape
    block = min(8, mode_count)
    kernel, token_specs, token = ordered(mix_kernel, after)
    return pl.pallas_call(
        kernel,
        grid=(mode_count // block,),
        in_specs=token_specs
        + [pl.BlockSpec((2, block, channels, channels), lambda g: (0, g, 0, 0))]
        * len(specs),
        out_specs=[pl.BlockSpec((block, 2 * channels, 2 * channels), lambda g: (g, 0, 0))]
        * len(specs),
        out_shape=[hbm(mode_count, 2 * channels, 2 * channels)] * len(specs),
        compiler_params=pltpu.CompilerParams(vmem_limit_bytes=VMEM_BYTES),
        cost_estimate=cost("mix", 0),
        name="mixing_matrices",
    )(*token, *in_hbm(specs))


def hbm(*shape):
    return pltpu.HBM(shape, jnp.bfloat16)


def in_hbm(arrays):
    return [pltpu.with_memory_space_constraint(array, pltpu.HBM) for array in arrays]


def cost(kernel, size):
    micros = COSTS.get(kernel, 3.0)
    return pl.CostEstimate(
        flops=int(micros * 1.15e9), bytes_accessed=int(size), transcendentals=0
    )


def ordered(kernel, after):
    if after is None:
        return kernel, [], []
    return (
        lambda _, *refs: kernel(*refs),
        [pl.BlockSpec(memory_space=pl.ANY)],
        in_hbm([after]),
    )


def mm(left, right, dims=(1, 0)):
    return lax.dot_general(
        left, right, (((dims[0],), (dims[1],)), ((), ())), preferred_element_type=jnp.float32
    )


def stack_rows(parts):
    if parts[0].shape[0] % 16 == 0:
        return jnp.concatenate(parts, axis=0)
    return jnp.concatenate([p.astype(jnp.float32) for p in parts], axis=0).astype(jnp.bfloat16)


def pack_kernel(x_ref, *refs):
    out_ref, wide = refs[-2:]
    channels, rows, ways, lanes = x_ref.shape
    wide[...] = x_ref[...].astype(jnp.float32).reshape(channels * rows * ways, lanes)
    for way in range(ways):
        picked = wide[pl.ds(way, channels * rows, stride=ways), :]
        out_ref[way] = picked.reshape(channels, rows, lanes).astype(jnp.bfloat16)


def pack(kernel_name, field, first, count, ways, after):
    channels, rows, _, lanes = field.shape
    depth = min(16, channels)
    return pl.pallas_call(
        pack_kernel,
        grid=(count, channels // depth),
        in_specs=[pl.BlockSpec((depth, rows, ways, lanes), lambda k, g: (g, 0, first + k, 0))]
        + [pl.BlockSpec(memory_space=pl.ANY)] * len(after),
        out_specs=pl.BlockSpec((ways, None, depth, rows, lanes), lambda k, g: (0, k, g, 0, 0)),
        out_shape=hbm(ways, count, channels, rows, lanes),
        scratch_shapes=[pltpu.VMEM((depth * rows * ways, lanes), jnp.float32)],
        compiler_params=pltpu.CompilerParams(vmem_limit_bytes=VMEM_BYTES),
        cost_estimate=cost(kernel_name, 0),
        name="pack_columns",
    )(*in_hbm([field, *after]))


def side_kernel(ways, me_ref, *refs):
    for x_ref, out_ref in zip(refs[:ways], refs[-ways:]):
        out_ref[...] = x_ref[...]


def rows_first(field, ways, me, after):
    channels, rows, cols, lanes = field.shape
    across = rows // ways

    def rows_of(step):
        return pl.BlockSpec(
            (channels, None, cols, lanes), lambda r, me: (0, (me[1] ^ step) * across + r, 0, 0)
        )

    return pl.pallas_call(
        functools.partial(side_kernel, ways),
        grid_spec=pltpu.PrefetchScalarGridSpec(
            num_scalar_prefetch=1,
            grid=(across,),
            in_specs=[rows_of(step) for step in range(ways)]
            + [pl.BlockSpec(memory_space=pl.ANY)],
            out_specs=[
                pl.BlockSpec((None, channels, cols, lanes), lambda r, me: (r, 0, 0, 0))
            ]
            * ways,
        ),
        out_shape=[hbm(across, channels, cols, lanes)] * ways,
        compiler_params=pltpu.CompilerParams(vmem_limit_bytes=VMEM_BYTES),
        cost_estimate=cost("rows", 0),
        name="rows_first",
    )(me, *in_hbm([field] * ways + [after]))


def mix_modes(mix_ref, spectra, mixed):
    mode_count, depth, _ = mix_ref.shape
    channels = depth // 2

    def one(mode, _):
        block = spectra[pl.ds(pl.multiple_of(mode * depth, depth), depth), :].astype(jnp.bfloat16)
        result = mm(mix_ref[mode], block)
        for part in range(2):
            mixed[pl.ds(part * mode_count + mode, channels, stride=2 * mode_count), :] = result[
                part * channels : (part + 1) * channels
            ]
        return 0

    lax.fori_loop(0, mode_count, one, 0, unroll=4)


def keep_spectra(spectra, result, channel, mode_count, channels, lanes):
    for at in range(2):
        for part in range(2):
            spectra[pl.ds(part * channels + channel + at, mode_count, stride=2 * channels), :] = (
                result[part * mode_count : (part + 1) * mode_count, at * lanes : (at + 1) * lanes]
            )


def mixed_pair(mixed, channel, coefs):
    start = pl.multiple_of(channel * coefs, 2 * coefs)
    return jnp.concatenate(
        [mixed[pl.ds(start, coefs), :], mixed[pl.ds(start + coefs, coefs), :]], axis=1
    ).astype(jnp.bfloat16)


def lines_kernel(ways, ft_ref, it_ref, mix_ref, *refs):
    refs, (spectra, mixed, wide) = refs[:-3], refs[-3:]
    if len(refs) == 2 * ways:
        pieces, outs = refs[:ways], [[out] for out in refs[ways:]]
    else:
        pieces = [refs[0].at[way] for way in range(ways)]
        outs = [[out.at[way] for out in refs[1:]] for way in range(ways)]
    channels, length, lanes = pieces[0].shape
    mode_count = mix_ref.shape[0]
    total = ways * length

    def forward(pair, _):
        channel = 2 * pair
        right = jnp.concatenate(
            [stack_rows([piece[channel + at] for piece in pieces]) for at in range(2)], axis=1
        )
        keep_spectra(spectra, mm(ft_ref[...], right), channel, mode_count, channels, lanes)
        return 0

    lax.fori_loop(0, channels // 2, forward, 0, unroll=4)
    mix_modes(mix_ref, spectra, mixed)

    def inverse(pair, _):
        channel = 2 * pair
        result = mm(it_ref[...], mixed_pair(mixed, channel, 2 * mode_count))
        for at in range(2):
            wide[pl.ds(channel + at, total, stride=channels), :] = result[
                :, at * lanes : (at + 1) * lanes
            ]
        return 0

    lax.fori_loop(0, channels // 2, inverse, 0, unroll=4)
    for step in range(ways):
        start = step * length
        for out in outs[step]:
            rows = out.shape[0]
            part = wide[pl.ds(start * channels, rows * channels), :]
            out[...] = part.reshape(rows, channels, lanes).astype(jnp.bfloat16)
            start += rows


def along_lines(
    kernel_name, pieces, weights, begin, count, after, me=None, groups=None, outs=None, done=(), held=()
):
    stacked = not isinstance(pieces, list)
    mode_count = weights.shape[0]
    if stacked:
        ways, several, channels, length, lanes = pieces.shape
        pieces = [pieces]
    else:
        ways = len(pieces)
        several, channels, length, lanes = pieces[0].shape
    total = ways * length
    forward = forward_rows(total, mode_count)
    back = inverse_rows(total, mode_count).T
    if stacked:
        back = back.reshape(ways, groups, length // groups, 2 * mode_count)
        back = back.swapaxes(1, 2).reshape(total, 2 * mode_count)
        in_spec = pl.BlockSpec(
            (ways, None, channels, length, lanes), lambda g: (0, begin + g, 0, 0, 0)
        )
        out_specs = [
            pl.BlockSpec((ways, cells, channels, lanes), lambda g, place=place: (0, place + g, 0, 0))
            for _, cells, place in outs
        ]
        out_shape = [hbm(ways, cells, channels, lanes) for cells, _, _ in outs]
    else:
        order = me ^ jnp.arange(ways)
        forward = forward.reshape(2 * mode_count, ways, length)
        forward = jnp.take(forward, order, axis=1).reshape(2 * mode_count, total)
        back = back.reshape(ways, length, 2 * mode_count)
        back = jnp.take(back, order, axis=0).reshape(total, 2 * mode_count)
        in_spec = pl.BlockSpec((None, channels, length, lanes), lambda g: (begin + g, 0, 0, 0))
        out_specs = [
            pl.BlockSpec((None, length, channels, lanes), lambda g: (begin + g, 0, 0, 0))
        ] * ways
        out_shape = [hbm(several, length, channels, lanes)] * ways
    whole = lambda shape: pl.BlockSpec(shape, lambda g: (0,) * len(shape))
    idle = [*done, *held, *after]
    aliases = {at: at for at in range(len(done))}
    aliases |= {len(done) + at: len(out_specs) + at for at in range(len(held))}
    last = len(idle) + 3 + len(pieces) + len(out_specs)
    elsewhere = pl.BlockSpec(memory_space=pl.ANY)
    return pl.pallas_call(
        lambda *refs: lines_kernel(ways, *refs[len(idle) : last], *refs[-3:]),
        grid=(count,),
        in_specs=[elsewhere] * len(idle)
        + [whole(forward.shape), whole(back.shape), whole(weights.shape)]
        + [in_spec] * len(pieces),
        out_specs=out_specs + [elsewhere] * len(held),
        out_shape=out_shape + [hbm(*array.shape) for array in held],
        input_output_aliases=aliases,
        scratch_shapes=[
            pltpu.VMEM((2 * channels * mode_count, lanes), jnp.float32),
            pltpu.VMEM((2 * channels * mode_count, lanes), jnp.float32),
            pltpu.VMEM((total * channels, lanes), jnp.float32),
        ],
        compiler_params=pltpu.CompilerParams(vmem_limit_bytes=VMEM_BYTES),
        cost_estimate=cost(kernel_name, 0),
        name="line_branch",
    )(*in_hbm(idle), forward, back, *in_hbm([weights, *pieces]))


def last_kernel(ft_ref, it_ref, mix_ref, x_ref, out_ref, spectra, mixed, wide):
    channels, rows, cols, length = x_ref.shape
    mode_count = mix_ref.shape[0]
    cells = rows * cols

    def forward(pair, _):
        channel = 2 * pair
        right = jnp.concatenate(
            [x_ref[channel + at].reshape(cells, length) for at in range(2)], axis=0
        )
        keep_spectra(
            spectra, mm(ft_ref[...], right, (1, 1)), channel, mode_count, channels, cells
        )
        return 0

    lax.fori_loop(0, channels // 2, forward, 0, unroll=4)
    mix_modes(mix_ref, spectra, mixed)

    def inverse(pair, _):
        channel = 2 * pair
        result = mm(mixed_pair(mixed, channel, 2 * mode_count), it_ref[...], (0, 0))
        for at in range(2):
            wide[pl.ds(channel + at, cells, stride=channels), :] = result[
                at * cells : (at + 1) * cells
            ]
        return 0

    lax.fori_loop(0, channels // 2, inverse, 0, unroll=4)
    out_ref[...] = wide[...].reshape(rows, cols, channels, length).astype(jnp.bfloat16)


def last_branch(kernel_name, field, weights, part, parts, done, after, held=()):
    channels, rows, cols, length = field.shape
    mode_count = weights.shape[0]
    block = max(1, min(rows // parts, 128 // cols))
    steps = rows // block // parts
    forward, back = forward_rows(length, mode_count), inverse_rows(length, mode_count)
    whole = lambda shape: pl.BlockSpec(shape, lambda g: (0,) * len(shape))
    elsewhere = pl.BlockSpec(memory_space=pl.ANY)
    kept = ([] if done is None else [done]) + list(held)
    moved = 1 if done is None else 0
    idle = kept + list(after)
    return pl.pallas_call(
        lambda *refs: last_kernel(*refs[len(idle) : len(idle) + 5], *refs[-3:]),
        grid=(steps,),
        in_specs=[elsewhere] * len(idle)
        + [
            whole(forward.shape),
            whole(back.shape),
            whole(weights.shape),
            pl.BlockSpec(
                (channels, block, cols, length), lambda g: (0, part * steps + g, 0, 0)
            ),
        ],
        out_specs=[
            pl.BlockSpec((block, cols, channels, length), lambda g: (part * steps + g, 0, 0, 0))
        ]
        + [elsewhere] * len(held),
        out_shape=[hbm(rows, cols, channels, length)] + [hbm(*array.shape) for array in held],
        input_output_aliases={at: moved + at for at in range(len(kept))},
        scratch_shapes=[
            pltpu.VMEM((2 * channels * mode_count, block * cols), jnp.float32),
            pltpu.VMEM((2 * channels * mode_count, block * cols), jnp.float32),
            pltpu.VMEM((block * cols * channels, length), jnp.float32),
        ],
        compiler_params=pltpu.CompilerParams(vmem_limit_bytes=VMEM_BYTES),
        cost_estimate=cost(kernel_name, 0),
        name="last_branch",
    )(*in_hbm(idle), forward, back, *in_hbm([weights, field]))


def cell_kernel(col_ways, me_ref, x_ref, win_ref, wout_ref, bin_ref, bout_ref, *refs):
    first_ref, second, third_ref = refs[0], refs[1 : 1 + col_ways], refs[1 + col_ways]
    out_ref, now, wide = refs[-3:]
    channels, _, ways, lanes = x_ref.shape

    for step in range(col_ways):

        @pl.when(pl.program_id(0) == step)
        def _():
            now[...] = second[step][...]

    for col in range(0, ways, 2):
        summed = []
        for at in range(2):
            pair = first_ref[col + at].astype(jnp.float32) + now[col + at].astype(jnp.float32)
            pair = pair.astype(jnp.bfloat16).astype(jnp.float32)
            total = pair + third_ref[col + at].astype(jnp.float32)
            summed.append(total.astype(jnp.bfloat16))
        pre = mm(win_ref[...], jnp.concatenate(summed, axis=1)) + bin_ref[...]
        hidden = (0.5 * pre * (1.0 + lax.erf(pre * HALF_ROOT))).astype(jnp.bfloat16)
        result = mm(wout_ref[...], hidden) + bout_ref[...]
        for at in range(2):
            wide[pl.ds(col + at, channels, stride=ways), :] = result[
                :, at * lanes : (at + 1) * lanes
            ]
    total = wide[...].reshape(channels, ways, lanes) + x_ref[:, 0].astype(jnp.float32)
    out_ref[:, 0] = total.astype(jnp.bfloat16)


def cells(kernel_name, field, first, base, second, third, ffn, chunk, begin, count, me, done, after):
    channels, rows, cols, lanes = field.shape
    ways, col_ways = first.shape[0], len(second)
    across = rows // col_ways

    def row(step, at, me):
        return (me[1] ^ step) * across + begin + at

    def own_row(which):
        def index(step, at, me):
            now = jnp.where(step == which, at, jnp.where(step < which, 0, count - 1))
            return begin + now, chunk, 0, 0

        return pl.BlockSpec((None, ways, channels, lanes), index)

    whole = lambda shape: pl.BlockSpec(shape, lambda *_: (0,) * len(shape))
    tile = pl.BlockSpec((channels, 1, ways, lanes), lambda s, a, me: (0, row(s, a, me), chunk, 0))
    in_specs = [tile] + [whole(w.shape) for w in ffn]
    in_specs.append(
        pl.BlockSpec(
            (ways, None, channels, lanes),
            lambda s, a, me: (0, base + a * col_ways + (me[1] ^ s), 0, 0),
        )
    )
    in_specs += [own_row(step) for step in range(col_ways)]
    in_specs.append(
        pl.BlockSpec((None, ways, channels, lanes), lambda s, a, me: (row(s, a, me), chunk, 0, 0))
    )
    operands = [me, *in_hbm([field]), *ffn, *in_hbm([first, *second, third])]
    aliases = {}
    if done is not None:
        aliases = {len(operands): 0}
    for array in (done, after):
        if array is not None:
            in_specs.append(pl.BlockSpec(memory_space=pl.ANY))
            operands += in_hbm([array])
    return pl.pallas_call(
        functools.partial(cell_kernel, col_ways),
        grid_spec=pltpu.PrefetchScalarGridSpec(
            num_scalar_prefetch=1,
            grid=(col_ways, count),
            in_specs=in_specs,
            out_specs=tile,
            scratch_shapes=[
                pltpu.VMEM((ways, channels, lanes), jnp.bfloat16),
                pltpu.VMEM((channels * ways, lanes), jnp.float32),
            ],
        ),
        out_shape=hbm(*field.shape),
        input_output_aliases=aliases,
        compiler_params=pltpu.CompilerParams(vmem_limit_bytes=VMEM_BYTES),
        cost_estimate=cost(kernel_name, 0),
        name="feed_forward",
    )(*operands)


def swap(piece, axis, step):
    ways = lax.axis_size(axis)
    return lax.ppermute(piece, axis, [(at, at ^ step) for at in range(ways)])


def exchange(pieces, axis):
    return [swap(piece, axis, step) if step else piece for step, piece in enumerate(pieces)]


def trade(stack):
    return lax.all_to_all(stack, "row", split_axis=0, concat_axis=0)


def body(field, spec_first, spec_second, spec_third, ffn_in, ffn_out, bias_in, bias_out):
    channels, rows, cols, lanes = field.shape
    ways, col_ways = lax.axis_size("row"), lax.axis_size("col")
    row_me, col_me = lax.axis_index("row"), lax.axis_index("col")
    me = jnp.stack([row_me, col_me]).astype(jnp.int32)
    chunks = cols // ways
    across = rows // col_ways
    ffn = (ffn_in.T, ffn_out.T, bias_in[:, None], bias_out[:, None])

    early_count = max(1, chunks // 2)
    rest = chunks - early_count
    early = pack("pack0", field, 0, early_count, ways, [])
    early_in = trade(early)
    side = rows_first(field, col_ways, me, early)
    side_in = exchange(side, "col")
    first_mix, second_mix, third_mix = mix_rows(side[0], spec_first, spec_second, spec_third)
    (third,) = last_branch("last0", field, third_mix, 0, 2, None, [])
    (third,) = last_branch("last1", field, third_mix, 1, 2, third, [])
    late_in = trade(pack("pack1", field, early_count, rest, ways, [third]))
    (parts,) = along_lines(
        "dim1",
        early_in,
        first_mix,
        0,
        early_count,
        [third],
        groups=col_ways,
        outs=[(early_count * rows, rows, 0)],
    )
    cut = across // 2
    second = along_lines("dim2a", side_in, second_mix, 0, cut, [parts], me=col_me)
    *second, parts = along_lines(
        "dim2b", side_in, second_mix, cut, across - cut, [], me=col_me, done=second, held=[parts]
    )
    second_in = exchange(second, "col")
    after = [second[0], *second_in[1:]]
    if rest == 2:
        half = rows // 2
        outs = [(rows + half, rows, 0)]
        (middle,) = along_lines(
            "late0", late_in, first_mix, 0, 1, after, groups=col_ways, outs=outs
        )
        outs = [(rows + half, half, rows // half), (half, half, 0)]
        middle, end = along_lines(
            "late1", late_in, first_mix, 1, 1, [], groups=col_ways, outs=outs, done=[middle]
        )
        back = [parts, middle, end]
    else:
        (late,) = along_lines(
            "late0", late_in, first_mix, 0, rest, after, groups=col_ways, outs=[(rest * rows, rows, 0)]
        )
        back = [parts, late]
    back = [trade(array) for array in back]

    calls = [(0, chunk * rows, chunk, 0, across) for chunk in range(early_count)]
    if rest == 2:
        calls.append((1, 0, early_count, 0, across))
        calls.append((1, rows, early_count + 1, 0, cut))
        calls.append((2, 0, early_count + 1, cut, across - cut))
    else:
        calls += [(1, at * rows, early_count + at, 0, across) for at in range(rest)]
    result, token = None, late_in if rest != 2 else end
    for at, (array, base, chunk, begin, count) in enumerate(calls):
        result = cells(
            f"ffn{at}",
            field,
            back[array],
            base,
            second_in,
            third,
            ffn,
            chunk,
            begin,
            count,
            me,
            result,
            token,
        )
        token = None
    return result


def solution(mesh):
    return jax.shard_map(
        body,
        mesh=mesh,
        in_specs=(P("grp", "row", "col", None), P(), P(), P(), P(), P(), P(), P()),
        out_specs=P("grp", "row", "col", None),
        check_vma=False,
    )
```

```python
import functools
import math

import jax
import jax.numpy as jnp
from jax import lax
from jax.experimental import pallas as pl
from jax.experimental.pallas import tpu as pltpu
from jax.sharding import PartitionSpec as P

MIB = 1024 * 1024
VMEM_BYTES = 62 * MIB
COSTS = {
    "pack0": 8.0,
    "pack1": 8.0,
    "rows": 7.6,
    "mix": 5.0,
    "last0": 22.0,
    "last1": 22.0,
    "dim1": 20.0,
    "dim2a": 20.0,
    "dim2b": 20.0,
    "late0": 200.0,
    "late1": 10.0,
    "ffn0": 2.0,
    "ffn1": 2.0,
    "ffn2": 60.0,
    "ffn3": 60.0,
    "ffn4": 11.0,
}
HALF_ROOT = math.sqrt(0.5)


def forward_rows(length, mode_count):
    grid_pos = jnp.arange(length, dtype=jnp.int32)[None, :]
    mode_location = jnp.arange(mode_count, dtype=jnp.int32)[:, None]
    phase = (grid_pos * mode_location % length).astype(jnp.float32) * (2.0 * math.pi / length)
    return jnp.concatenate([jnp.cos(phase), -jnp.sin(phase)], axis=0).astype(jnp.bfloat16)


def inverse_rows(length, mode_count):
    mode_location = jnp.arange(mode_count, dtype=jnp.int32)[:, None]
    grid_pos = jnp.arange(length, dtype=jnp.int32)[None, :]
    phase = (grid_pos * mode_location % length).astype(jnp.float32) * (2.0 * math.pi / length)
    factor = jnp.where(mode_location == 0, 1.0, 2.0).astype(jnp.float32) / length
    return jnp.concatenate(
        [factor * jnp.cos(phase), -factor * jnp.sin(phase)], axis=0
    ).astype(jnp.bfloat16)


def mix_kernel(*refs):
    count = len(refs) // 2
    for spec, out in zip(refs[:count], refs[count:]):
        channels = spec.shape[-1]
        for mode in range(spec.shape[1]):
            real = spec[0, mode].astype(jnp.float32).T
            imag = spec[1, mode].astype(jnp.float32).T
            upper = jnp.concatenate([real, -imag], axis=1)
            lower = jnp.concatenate([imag, real], axis=1)
            out[mode, :channels] = upper.astype(jnp.bfloat16)
            out[mode, channels:] = lower.astype(jnp.bfloat16)


def mix_rows(after, *specs):
    _, mode_count, channels, _ = specs[0].shape
    block = min(8, mode_count)
    kernel, token_specs, token = ordered(mix_kernel, after)
    return pl.pallas_call(
        kernel,
        grid=(mode_count // block,),
        in_specs=token_specs
        + [pl.BlockSpec((2, block, channels, channels), lambda g: (0, g, 0, 0))]
        * len(specs),
        out_specs=[pl.BlockSpec((block, 2 * channels, 2 * channels), lambda g: (g, 0, 0))]
        * len(specs),
        out_shape=[hbm(mode_count, 2 * channels, 2 * channels)] * len(specs),
        compiler_params=pltpu.CompilerParams(vmem_limit_bytes=VMEM_BYTES),
        cost_estimate=cost("mix", 0),
        name="mixing_matrices",
    )(*token, *in_hbm(specs))


def hbm(*shape):
    return pltpu.HBM(shape, jnp.bfloat16)


def in_hbm(arrays):
    return [pltpu.with_memory_space_constraint(array, pltpu.HBM) for array in arrays]


def cost(kernel, size):
    micros = COSTS.get(kernel, 3.0)
    return pl.CostEstimate(
        flops=int(micros * 1.15e9), bytes_accessed=int(size), transcendentals=0
    )


def ordered(kernel, after):
    if after is None:
        return kernel, [], []
    return (
        lambda _, *refs: kernel(*refs),
        [pl.BlockSpec(memory_space=pl.ANY)],
        in_hbm([after]),
    )


def mm(left, right, dims=(1, 0)):
    return lax.dot_general(
        left, right, (((dims[0],), (dims[1],)), ((), ())), preferred_element_type=jnp.float32
    )


def stack_rows(parts):
    if parts[0].shape[0] % 16 == 0:
        return jnp.concatenate(parts, axis=0)
    return jnp.concatenate([p.astype(jnp.float32) for p in parts], axis=0).astype(jnp.bfloat16)


def pack_kernel(x_ref, *refs):
    out_ref, wide = refs[-2:]
    channels, rows, ways, lanes = x_ref.shape
    wide[...] = x_ref[...].astype(jnp.float32).reshape(channels * rows * ways, lanes)
    for way in range(ways):
        picked = wide[pl.ds(way, channels * rows, stride=ways), :]
        out_ref[way] = picked.reshape(channels, rows, lanes).astype(jnp.bfloat16)


def pack(kernel_name, field, first, count, ways, after):
    channels, rows, _, lanes = field.shape
    depth = min(16, channels)
    return pl.pallas_call(
        pack_kernel,
        grid=(count, channels // depth),
        in_specs=[pl.BlockSpec((depth, rows, ways, lanes), lambda k, g: (g, 0, first + k, 0))]
        + [pl.BlockSpec(memory_space=pl.ANY)] * len(after),
        out_specs=pl.BlockSpec((ways, None, depth, rows, lanes), lambda k, g: (0, k, g, 0, 0)),
        out_shape=hbm(ways, count, channels, rows, lanes),
        scratch_shapes=[pltpu.VMEM((depth * rows * ways, lanes), jnp.float32)],
        compiler_params=pltpu.CompilerParams(vmem_limit_bytes=VMEM_BYTES),
        cost_estimate=cost(kernel_name, 0),
        name="pack_columns",
    )(*in_hbm([field, *after]))


def side_kernel(ways, me_ref, *refs):
    for x_ref, out_ref in zip(refs[:ways], refs[-ways:]):
        out_ref[...] = x_ref[...]


def rows_first(field, ways, me, after):
    channels, rows, cols, lanes = field.shape
    across = rows // ways

    def rows_of(step):
        return pl.BlockSpec(
            (channels, None, cols, lanes), lambda r, me: (0, (me[1] ^ step) * across + r, 0, 0)
        )

    return pl.pallas_call(
        functools.partial(side_kernel, ways),
        grid_spec=pltpu.PrefetchScalarGridSpec(
            num_scalar_prefetch=1,
            grid=(across,),
            in_specs=[rows_of(step) for step in range(ways)]
            + [pl.BlockSpec(memory_space=pl.ANY)],
            out_specs=[
                pl.BlockSpec((None, channels, cols, lanes), lambda r, me: (r, 0, 0, 0))
            ]
            * ways,
        ),
        out_shape=[hbm(across, channels, cols, lanes)] * ways,
        compiler_params=pltpu.CompilerParams(vmem_limit_bytes=VMEM_BYTES),
        cost_estimate=cost("rows", 0),
        name="rows_first",
    )(me, *in_hbm([field] * ways + [after]))


def mix_modes(mix_ref, spectra, mixed):
    mode_count, depth, _ = mix_ref.shape
    channels = depth // 2

    def one(mode, _):
        block = spectra[pl.ds(pl.multiple_of(mode * depth, depth), depth), :].astype(jnp.bfloat16)
        result = mm(mix_ref[mode], block)
        for part in range(2):
            mixed[pl.ds(part * mode_count + mode, channels, stride=2 * mode_count), :] = result[
                part * channels : (part + 1) * channels
            ]
        return 0

    lax.fori_loop(0, mode_count, one, 0, unroll=4)


def keep_spectra(spectra, result, channel, mode_count, channels, lanes):
    for at in range(2):
        for part in range(2):
            spectra[pl.ds(part * channels + channel + at, mode_count, stride=2 * channels), :] = (
                result[part * mode_count : (part + 1) * mode_count, at * lanes : (at + 1) * lanes]
            )


def mixed_pair(mixed, channel, coefs):
    start = pl.multiple_of(channel * coefs, 2 * coefs)
    return jnp.concatenate(
        [mixed[pl.ds(start, coefs), :], mixed[pl.ds(start + coefs, coefs), :]], axis=1
    ).astype(jnp.bfloat16)


def lines_kernel(ways, ft_ref, it_ref, mix_ref, *refs):
    refs, (spectra, mixed, wide) = refs[:-3], refs[-3:]
    if len(refs) == 2 * ways:
        pieces, outs = refs[:ways], [[out] for out in refs[ways:]]
    else:
        pieces = [refs[0].at[way] for way in range(ways)]
        outs = [[out.at[way] for out in refs[1:]] for way in range(ways)]
    channels, length, lanes = pieces[0].shape
    mode_count = mix_ref.shape[0]
    total = ways * length

    def forward(pair, _):
        channel = 2 * pair
        right = jnp.concatenate(
            [stack_rows([piece[channel + at] for piece in pieces]) for at in range(2)], axis=1
        )
        keep_spectra(spectra, mm(ft_ref[...], right), channel, mode_count, channels, lanes)
        return 0

    lax.fori_loop(0, channels // 2, forward, 0, unroll=4)
    mix_modes(mix_ref, spectra, mixed)

    def inverse(pair, _):
        channel = 2 * pair
        result = mm(it_ref[...], mixed_pair(mixed, channel, 2 * mode_count))
        for at in range(2):
            wide[pl.ds(channel + at, total, stride=channels), :] = result[
                :, at * lanes : (at + 1) * lanes
            ]
        return 0

    lax.fori_loop(0, channels // 2, inverse, 0, unroll=4)
    for step in range(ways):
        start = step * length
        for out in outs[step]:
            rows = out.shape[0]
            part = wide[pl.ds(start * channels, rows * channels), :]
            out[...] = part.reshape(rows, channels, lanes).astype(jnp.bfloat16)
            start += rows


def along_lines(
    kernel_name, pieces, weights, begin, count, after, me=None, groups=None, outs=None, done=(), held=()
):
    stacked = not isinstance(pieces, list)
    mode_count = weights.shape[0]
    if stacked:
        ways, several, channels, length, lanes = pieces.shape
        pieces = [pieces]
    else:
        ways = len(pieces)
        several, channels, length, lanes = pieces[0].shape
    total = ways * length
    forward = forward_rows(total, mode_count)
    back = inverse_rows(total, mode_count).T
    if stacked:
        back = back.reshape(ways, groups, length // groups, 2 * mode_count)
        back = back.swapaxes(1, 2).reshape(total, 2 * mode_count)
        in_spec = pl.BlockSpec(
            (ways, None, channels, length, lanes), lambda g: (0, begin + g, 0, 0, 0)
        )
        out_specs = [
            pl.BlockSpec((ways, cells, channels, lanes), lambda g, place=place: (0, place + g, 0, 0))
            for _, cells, place in outs
        ]
        out_shape = [hbm(ways, cells, channels, lanes) for cells, _, _ in outs]
    else:
        order = me ^ jnp.arange(ways)
        forward = forward.reshape(2 * mode_count, ways, length)
        forward = jnp.take(forward, order, axis=1).reshape(2 * mode_count, total)
        back = back.reshape(ways, length, 2 * mode_count)
        back = jnp.take(back, order, axis=0).reshape(total, 2 * mode_count)
        in_spec = pl.BlockSpec((None, channels, length, lanes), lambda g: (begin + g, 0, 0, 0))
        out_specs = [
            pl.BlockSpec((None, length, channels, lanes), lambda g: (begin + g, 0, 0, 0))
        ] * ways
        out_shape = [hbm(several, length, channels, lanes)] * ways
    whole = lambda shape: pl.BlockSpec(shape, lambda g: (0,) * len(shape))
    idle = [*done, *held, *after]
    aliases = {at: at for at in range(len(done))}
    aliases |= {len(done) + at: len(out_specs) + at for at in range(len(held))}
    last = len(idle) + 3 + len(pieces) + len(out_specs)
    elsewhere = pl.BlockSpec(memory_space=pl.ANY)
    return pl.pallas_call(
        lambda *refs: lines_kernel(ways, *refs[len(idle) : last], *refs[-3:]),
        grid=(count,),
        in_specs=[elsewhere] * len(idle)
        + [whole(forward.shape), whole(back.shape), whole(weights.shape)]
        + [in_spec] * len(pieces),
        out_specs=out_specs + [elsewhere] * len(held),
        out_shape=out_shape + [hbm(*array.shape) for array in held],
        input_output_aliases=aliases,
        scratch_shapes=[
            pltpu.VMEM((2 * channels * mode_count, lanes), jnp.float32),
            pltpu.VMEM((2 * channels * mode_count, lanes), jnp.float32),
            pltpu.VMEM((total * channels, lanes), jnp.float32),
        ],
        compiler_params=pltpu.CompilerParams(vmem_limit_bytes=VMEM_BYTES),
        cost_estimate=cost(kernel_name, 0),
        name="line_branch",
    )(*in_hbm(idle), forward, back, *in_hbm([weights, *pieces]))


def last_kernel(ft_ref, it_ref, mix_ref, x_ref, out_ref, spectra, mixed, wide):
    channels, rows, cols, length = x_ref.shape
    mode_count = mix_ref.shape[0]
    cells = rows * cols

    def forward(pair, _):
        channel = 2 * pair
        right = jnp.concatenate(
            [x_ref[channel + at].reshape(cells, length) for at in range(2)], axis=0
        )
        keep_spectra(
            spectra, mm(ft_ref[...], right, (1, 1)), channel, mode_count, channels, cells
        )
        return 0

    lax.fori_loop(0, channels // 2, forward, 0, unroll=4)
    mix_modes(mix_ref, spectra, mixed)

    def inverse(pair, _):
        channel = 2 * pair
        result = mm(mixed_pair(mixed, channel, 2 * mode_count), it_ref[...], (0, 0))
        for at in range(2):
            wide[pl.ds(channel + at, cells, stride=channels), :] = result[
                at * cells : (at + 1) * cells
            ]
        return 0

    lax.fori_loop(0, channels // 2, inverse, 0, unroll=4)
    out_ref[...] = wide[...].reshape(rows, cols, channels, length).astype(jnp.bfloat16)


def last_branch(kernel_name, field, weights, part, parts, done, after, held=()):
    channels, rows, cols, length = field.shape
    mode_count = weights.shape[0]
    block = max(1, min(rows // parts, 128 // cols))
    steps = rows // block // parts
    forward, back = forward_rows(length, mode_count), inverse_rows(length, mode_count)
    whole = lambda shape: pl.BlockSpec(shape, lambda g: (0,) * len(shape))
    elsewhere = pl.BlockSpec(memory_space=pl.ANY)
    kept = ([] if done is None else [done]) + list(held)
    moved = 1 if done is None else 0
    idle = kept + list(after)
    return pl.pallas_call(
        lambda *refs: last_kernel(*refs[len(idle) : len(idle) + 5], *refs[-3:]),
        grid=(steps,),
        in_specs=[elsewhere] * len(idle)
        + [
            whole(forward.shape),
            whole(back.shape),
            whole(weights.shape),
            pl.BlockSpec(
                (channels, block, cols, length), lambda g: (0, part * steps + g, 0, 0)
            ),
        ],
        out_specs=[
            pl.BlockSpec((block, cols, channels, length), lambda g: (part * steps + g, 0, 0, 0))
        ]
        + [elsewhere] * len(held),
        out_shape=[hbm(rows, cols, channels, length)] + [hbm(*array.shape) for array in held],
        input_output_aliases={at: moved + at for at in range(len(kept))},
        scratch_shapes=[
            pltpu.VMEM((2 * channels * mode_count, block * cols), jnp.float32),
            pltpu.VMEM((2 * channels * mode_count, block * cols), jnp.float32),
            pltpu.VMEM((block * cols * channels, length), jnp.float32),
        ],
        compiler_params=pltpu.CompilerParams(vmem_limit_bytes=VMEM_BYTES),
        cost_estimate=cost(kernel_name, 0),
        name="last_branch",
    )(*in_hbm(idle), forward, back, *in_hbm([weights, field]))


def cell_kernel(col_ways, me_ref, x_ref, win_ref, wout_ref, bin_ref, bout_ref, *refs):
    first_ref, second, third_ref = refs[0], refs[1 : 1 + col_ways], refs[1 + col_ways]
    out_ref, now, wide = refs[-3:]
    channels, rows, ways, lanes = x_ref.shape

    for step in range(col_ways):

        @pl.when(pl.program_id(0) == step)
        def _():
            now[...] = second[step][...]

    for row in range(rows):
        for col in range(0, ways, 2):
            summed = []
            for place in (col, col + 1):
                pair = first_ref[place, row].astype(jnp.float32)
                pair = (pair + now[row, place].astype(jnp.float32)).astype(jnp.bfloat16)
                total = pair.astype(jnp.float32) + third_ref[row, place].astype(jnp.float32)
                summed.append(total.astype(jnp.bfloat16))
            scaled = mm(win_ref[...], jnp.concatenate(summed, axis=1)) * HALF_ROOT + bin_ref[...]
            hidden = (scaled + scaled * lax.erf(scaled)).astype(jnp.bfloat16)
            result = mm(wout_ref[...], hidden) * HALF_ROOT + bout_ref[...]
            for at in range(2):
                wide[row, pl.ds(col + at, channels, stride=ways), :] = result[
                    :, at * lanes : (at + 1) * lanes
                ]
        total = wide[row].reshape(channels, ways, lanes) + x_ref[:, row].astype(jnp.float32)
        out_ref[:, row] = total.astype(jnp.bfloat16)


def cells(kernel_name, field, first, base, second, third, ffn, chunk, begin, count, me, done, after):
    channels, rows, cols, lanes = field.shape
    ways, col_ways = first.shape[0], len(second)
    across = rows // col_ways
    block = across // 2
    first = first.reshape(ways, -1, col_ways, channels, lanes)
    base, begin, steps = base // (col_ways * block), begin // block, count // block

    def row(step, at, me):
        return (me[1] ^ step) * (across // block) + begin + at

    def own_row(which):
        def index(step, at, me):
            now = jnp.where(step == which, at, jnp.where(step < which, 0, steps - 1))
            return begin + now, chunk, 0, 0

        return pl.BlockSpec((block, ways, channels, lanes), index)

    whole = lambda shape: pl.BlockSpec(shape, lambda *_: (0,) * len(shape))
    tile = pl.BlockSpec(
        (channels, block, ways, lanes), lambda s, a, me: (0, row(s, a, me), chunk, 0)
    )
    in_specs = [tile] + [whole(w.shape) for w in ffn]
    in_specs.append(
        pl.BlockSpec(
            (ways, block, None, channels, lanes),
            lambda s, a, me: (0, base + a, me[1] ^ s, 0, 0),
        )
    )
    in_specs += [own_row(step) for step in range(col_ways)]
    in_specs.append(
        pl.BlockSpec((block, ways, channels, lanes), lambda s, a, me: (row(s, a, me), chunk, 0, 0))
    )
    operands = [me, *in_hbm([field]), *ffn, *in_hbm([first, *second, third])]
    aliases = {}
    if done is not None:
        aliases = {len(operands): 0}
    for array in (done, after):
        if array is not None:
            in_specs.append(pl.BlockSpec(memory_space=pl.ANY))
            operands += in_hbm([array])
    return pl.pallas_call(
        functools.partial(cell_kernel, col_ways),
        grid_spec=pltpu.PrefetchScalarGridSpec(
            num_scalar_prefetch=1,
            grid=(col_ways, steps),
            in_specs=in_specs,
            out_specs=tile,
            scratch_shapes=[
                pltpu.VMEM((block, ways, channels, lanes), jnp.bfloat16),
                pltpu.VMEM((block, channels * ways, lanes), jnp.float32),
            ],
        ),
        out_shape=hbm(*field.shape),
        input_output_aliases=aliases,
        compiler_params=pltpu.CompilerParams(vmem_limit_bytes=VMEM_BYTES),
        cost_estimate=cost(kernel_name, 0),
        name="feed_forward",
    )(*operands)


def swap(piece, axis, step):
    ways = lax.axis_size(axis)
    return lax.ppermute(piece, axis, [(at, at ^ step) for at in range(ways)])


def exchange(pieces, axis):
    return [swap(piece, axis, step) if step else piece for step, piece in enumerate(pieces)]


def trade(stack):
    return lax.all_to_all(stack, "row", split_axis=0, concat_axis=0)


def body(field, spec_first, spec_second, spec_third, ffn_in, ffn_out, bias_in, bias_out):
    channels, rows, cols, lanes = field.shape
    ways, col_ways = lax.axis_size("row"), lax.axis_size("col")
    row_me, col_me = lax.axis_index("row"), lax.axis_index("col")
    me = jnp.stack([row_me, col_me]).astype(jnp.int32)
    chunks = cols // ways
    across = rows // col_ways
    ffn = (ffn_in.T, ffn_out.T, bias_in[:, None] * HALF_ROOT, bias_out[:, None])

    early_count = max(1, chunks // 2)
    rest = chunks - early_count
    early = pack("pack0", field, 0, early_count, ways, [])
    early_in = trade(early)
    side = rows_first(field, col_ways, me, early)
    side_in = exchange(side, "col")
    first_mix, second_mix, third_mix = mix_rows(side[0], spec_first, spec_second, spec_third)
    (third,) = last_branch("last0", field, third_mix, 0, 2, None, [])
    (third,) = last_branch("last1", field, third_mix, 1, 2, third, [])
    late_in = trade(pack("pack1", field, early_count, rest, ways, [third]))
    (parts,) = along_lines(
        "dim1",
        early_in,
        first_mix,
        0,
        early_count,
        [third],
        groups=col_ways,
        outs=[(early_count * rows, rows, 0)],
    )
    cut = across // 2
    second = along_lines("dim2a", side_in, second_mix, 0, cut, [parts], me=col_me)
    *second, parts = along_lines(
        "dim2b", side_in, second_mix, cut, across - cut, [], me=col_me, done=second, held=[parts]
    )
    second_in = exchange(second, "col")
    after = [second[0], *second_in[1:]]
    if rest == 2:
        half = rows // 2
        outs = [(rows + half, rows, 0)]
        (middle,) = along_lines(
            "late0", late_in, first_mix, 0, 1, after, groups=col_ways, outs=outs
        )
        outs = [(rows + half, half, rows // half), (half, half, 0)]
        middle, end = along_lines(
            "late1", late_in, first_mix, 1, 1, [], groups=col_ways, outs=outs, done=[middle]
        )
        back = [parts, middle, end]
    else:
        (late,) = along_lines(
            "late0", late_in, first_mix, 0, rest, after, groups=col_ways, outs=[(rest * rows, rows, 0)]
        )
        back = [parts, late]
    back = [trade(array) for array in back]

    calls = [(0, chunk * rows, chunk, 0, across) for chunk in range(early_count)]
    if rest == 2:
        calls.append((1, 0, early_count, 0, across))
        calls.append((1, rows, early_count + 1, 0, cut))
        calls.append((2, 0, early_count + 1, cut, across - cut))
    else:
        calls += [(1, at * rows, early_count + at, 0, across) for at in range(rest)]
    result, token = None, late_in if rest != 2 else end
    for at, (array, base, chunk, begin, count) in enumerate(calls):
        result = cells(
            f"ffn{at}",
            field,
            back[array],
            base,
            second_in,
            third,
            ffn,
            chunk,
            begin,
            count,
            me,
            result,
            token,
        )
        token = None
    return result


def solution(mesh):
    return jax.shard_map(
        body,
        mesh=mesh,
        in_specs=(P("grp", "row", "col", None), P(), P(), P(), P(), P(), P(), P()),
        out_specs=P("grp", "row", "col", None),
        check_vma=False,
    )
```

```python
import functools
import math

import jax
import jax.numpy as jnp
from jax import lax
from jax.experimental import pallas as pl
from jax.experimental.pallas import tpu as pltpu
from jax.sharding import PartitionSpec as P

MIB = 1024 * 1024
VMEM_BYTES = 62 * MIB
COSTS = {
    "pack0": 8.0,
    "pack1": 8.0,
    "rows": 7.6,
    "mix": 5.0,
    "last0": 22.0,
    "last1": 22.0,
    "dim1": 20.0,
    "dim2a": 20.0,
    "dim2b": 20.0,
    "late0": 200.0,
    "late1": 10.0,
    "ffn0": 2.0,
    "ffn1": 2.0,
    "ffn2": 60.0,
    "ffn3": 60.0,
    "ffn4": 11.0,
}
HALF_ROOT = math.sqrt(0.5)


def forward_rows(length, mode_count):
    grid_pos = jnp.arange(length, dtype=jnp.int32)[None, :]
    mode_location = jnp.arange(mode_count, dtype=jnp.int32)[:, None]
    phase = (grid_pos * mode_location % length).astype(jnp.float32) * (2.0 * math.pi / length)
    return jnp.concatenate([jnp.cos(phase), -jnp.sin(phase)], axis=0).astype(jnp.bfloat16)


def inverse_rows(length, mode_count):
    mode_location = jnp.arange(mode_count, dtype=jnp.int32)[:, None]
    grid_pos = jnp.arange(length, dtype=jnp.int32)[None, :]
    phase = (grid_pos * mode_location % length).astype(jnp.float32) * (2.0 * math.pi / length)
    factor = jnp.where(mode_location == 0, 1.0, 2.0).astype(jnp.float32) / length
    return jnp.concatenate(
        [factor * jnp.cos(phase), -factor * jnp.sin(phase)], axis=0
    ).astype(jnp.bfloat16)


def mix_kernel(*refs):
    count = len(refs) // 2
    for spec, out in zip(refs[:count], refs[count:]):
        channels = spec.shape[-1]
        for mode in range(spec.shape[1]):
            real = spec[0, mode].astype(jnp.float32).T
            imag = spec[1, mode].astype(jnp.float32).T
            upper = jnp.concatenate([real, -imag], axis=1)
            lower = jnp.concatenate([imag, real], axis=1)
            out[mode, :channels] = upper.astype(jnp.bfloat16)
            out[mode, channels:] = lower.astype(jnp.bfloat16)


def mix_rows(after, *specs):
    _, mode_count, channels, _ = specs[0].shape
    block = min(8, mode_count)
    kernel, token_specs, token = ordered(mix_kernel, after)
    return pl.pallas_call(
        kernel,
        grid=(mode_count // block,),
        in_specs=token_specs
        + [pl.BlockSpec((2, block, channels, channels), lambda g: (0, g, 0, 0))]
        * len(specs),
        out_specs=[pl.BlockSpec((block, 2 * channels, 2 * channels), lambda g: (g, 0, 0))]
        * len(specs),
        out_shape=[hbm(mode_count, 2 * channels, 2 * channels)] * len(specs),
        compiler_params=pltpu.CompilerParams(vmem_limit_bytes=VMEM_BYTES),
        cost_estimate=cost("mix", 0),
        name="mixing_matrices",
    )(*token, *in_hbm(specs))


def hbm(*shape):
    return pltpu.HBM(shape, jnp.bfloat16)


def in_hbm(arrays):
    return [pltpu.with_memory_space_constraint(array, pltpu.HBM) for array in arrays]


def cost(kernel, size):
    micros = COSTS.get(kernel, 3.0)
    return pl.CostEstimate(
        flops=int(micros * 1.15e9), bytes_accessed=int(size), transcendentals=0
    )


def ordered(kernel, after):
    if after is None:
        return kernel, [], []
    return (
        lambda _, *refs: kernel(*refs),
        [pl.BlockSpec(memory_space=pl.ANY)],
        in_hbm([after]),
    )


def mm(left, right, dims=(1, 0)):
    return lax.dot_general(
        left, right, (((dims[0],), (dims[1],)), ((), ())), preferred_element_type=jnp.float32
    )


def stack_rows(parts):
    if parts[0].shape[0] % 16 == 0:
        return jnp.concatenate(parts, axis=0)
    return jnp.concatenate([p.astype(jnp.float32) for p in parts], axis=0).astype(jnp.bfloat16)


def pack_kernel(x_ref, *refs):
    out_ref, wide = refs[-2:]
    channels, rows, ways, lanes = x_ref.shape
    wide[...] = x_ref[...].astype(jnp.float32).reshape(channels * rows * ways, lanes)
    for way in range(ways):
        picked = wide[pl.ds(way, channels * rows, stride=ways), :]
        out_ref[way] = picked.reshape(channels, rows, lanes).astype(jnp.bfloat16)


def pack(kernel_name, field, first, count, ways, after):
    channels, rows, _, lanes = field.shape
    depth = min(16, channels)
    return pl.pallas_call(
        pack_kernel,
        grid=(count, channels // depth),
        in_specs=[pl.BlockSpec((depth, rows, ways, lanes), lambda k, g: (g, 0, first + k, 0))]
        + [pl.BlockSpec(memory_space=pl.ANY)] * len(after),
        out_specs=pl.BlockSpec((ways, None, depth, rows, lanes), lambda k, g: (0, k, g, 0, 0)),
        out_shape=hbm(ways, count, channels, rows, lanes),
        scratch_shapes=[pltpu.VMEM((depth * rows * ways, lanes), jnp.float32)],
        compiler_params=pltpu.CompilerParams(vmem_limit_bytes=VMEM_BYTES),
        cost_estimate=cost(kernel_name, 0),
        name="pack_columns",
    )(*in_hbm([field, *after]))


def side_kernel(ways, me_ref, *refs):
    for x_ref, out_ref in zip(refs[:ways], refs[-ways:]):
        out_ref[...] = x_ref[...]


def rows_first(field, ways, me, after):
    channels, rows, cols, lanes = field.shape
    across = rows // ways

    def rows_of(step):
        return pl.BlockSpec(
            (channels, None, cols, lanes), lambda r, me: (0, (me[1] ^ step) * across + r, 0, 0)
        )

    return pl.pallas_call(
        functools.partial(side_kernel, ways),
        grid_spec=pltpu.PrefetchScalarGridSpec(
            num_scalar_prefetch=1,
            grid=(across,),
            in_specs=[rows_of(step) for step in range(ways)]
            + [pl.BlockSpec(memory_space=pl.ANY)],
            out_specs=[
                pl.BlockSpec((None, channels, cols, lanes), lambda r, me: (r, 0, 0, 0))
            ]
            * ways,
        ),
        out_shape=[hbm(across, channels, cols, lanes)] * ways,
        compiler_params=pltpu.CompilerParams(vmem_limit_bytes=VMEM_BYTES),
        cost_estimate=cost("rows", 0),
        name="rows_first",
    )(me, *in_hbm([field] * ways + [after]))


def mix_modes(mix_ref, spectra, mixed):
    mode_count, depth, _ = mix_ref.shape
    channels = depth // 2

    def one(mode, _):
        block = spectra[pl.ds(pl.multiple_of(mode * depth, depth), depth), :].astype(jnp.bfloat16)
        result = mm(mix_ref[mode], block)
        for part in range(2):
            mixed[pl.ds(part * mode_count + mode, channels, stride=2 * mode_count), :] = result[
                part * channels : (part + 1) * channels
            ]
        return 0

    lax.fori_loop(0, mode_count, one, 0, unroll=4)


def keep_spectra(spectra, result, channel, mode_count, channels, lanes):
    for at in range(2):
        for part in range(2):
            spectra[pl.ds(part * channels + channel + at, mode_count, stride=2 * channels), :] = (
                result[part * mode_count : (part + 1) * mode_count, at * lanes : (at + 1) * lanes]
            )


def mixed_pair(mixed, channel, coefs):
    start = pl.multiple_of(channel * coefs, 2 * coefs)
    return jnp.concatenate(
        [mixed[pl.ds(start, coefs), :], mixed[pl.ds(start + coefs, coefs), :]], axis=1
    ).astype(jnp.bfloat16)


def lines_kernel(ways, ft_ref, it_ref, mix_ref, *refs):
    refs, (spectra, mixed, wide) = refs[:-3], refs[-3:]
    if len(refs) == 2 * ways:
        pieces, outs = refs[:ways], [[out] for out in refs[ways:]]
    else:
        pieces = [refs[0].at[way] for way in range(ways)]
        outs = [[out.at[way] for out in refs[1:]] for way in range(ways)]
    channels, length, lanes = pieces[0].shape
    mode_count = mix_ref.shape[0]
    total = ways * length

    def forward(pair, _):
        channel = 2 * pair
        right = jnp.concatenate(
            [stack_rows([piece[channel + at] for piece in pieces]) for at in range(2)], axis=1
        )
        keep_spectra(spectra, mm(ft_ref[...], right), channel, mode_count, channels, lanes)
        return 0

    lax.fori_loop(0, channels // 2, forward, 0, unroll=4)
    mix_modes(mix_ref, spectra, mixed)

    def inverse(pair, _):
        channel = 2 * pair
        result = mm(it_ref[...], mixed_pair(mixed, channel, 2 * mode_count))
        for at in range(2):
            wide[pl.ds(channel + at, total, stride=channels), :] = result[
                :, at * lanes : (at + 1) * lanes
            ]
        return 0

    lax.fori_loop(0, channels // 2, inverse, 0, unroll=4)
    for step in range(ways):
        start = step * length
        for out in outs[step]:
            rows = out.shape[0]
            part = wide[pl.ds(start * channels, rows * channels), :]
            out[...] = part.reshape(rows, channels, lanes).astype(jnp.bfloat16)
            start += rows


def along_lines(
    kernel_name, pieces, weights, begin, count, after, me=None, groups=None, outs=None, done=(), held=()
):
    stacked = not isinstance(pieces, list)
    mode_count = weights.shape[0]
    if stacked:
        ways, several, channels, length, lanes = pieces.shape
        pieces = [pieces]
    else:
        ways = len(pieces)
        several, channels, length, lanes = pieces[0].shape
    total = ways * length
    forward = forward_rows(total, mode_count)
    back = inverse_rows(total, mode_count).T
    if stacked:
        back = back.reshape(ways, groups, length // groups, 2 * mode_count)
        back = back.swapaxes(1, 2).reshape(total, 2 * mode_count)
        in_spec = pl.BlockSpec(
            (ways, None, channels, length, lanes), lambda g: (0, begin + g, 0, 0, 0)
        )
        out_specs = [
            pl.BlockSpec((ways, cells, channels, lanes), lambda g, place=place: (0, place + g, 0, 0))
            for _, cells, place in outs
        ]
        out_shape = [hbm(ways, cells, channels, lanes) for cells, _, _ in outs]
    else:
        order = me ^ jnp.arange(ways)
        forward = forward.reshape(2 * mode_count, ways, length)
        forward = jnp.take(forward, order, axis=1).reshape(2 * mode_count, total)
        back = back.reshape(ways, length, 2 * mode_count)
        back = jnp.take(back, order, axis=0).reshape(total, 2 * mode_count)
        in_spec = pl.BlockSpec((None, channels, length, lanes), lambda g: (begin + g, 0, 0, 0))
        out_specs = [
            pl.BlockSpec((None, length, channels, lanes), lambda g: (begin + g, 0, 0, 0))
        ] * ways
        out_shape = [hbm(several, length, channels, lanes)] * ways
    whole = lambda shape: pl.BlockSpec(shape, lambda g: (0,) * len(shape))
    idle = [*done, *held, *after]
    aliases = {at: at for at in range(len(done))}
    aliases |= {len(done) + at: len(out_specs) + at for at in range(len(held))}
    last = len(idle) + 3 + len(pieces) + len(out_specs)
    elsewhere = pl.BlockSpec(memory_space=pl.ANY)
    return pl.pallas_call(
        lambda *refs: lines_kernel(ways, *refs[len(idle) : last], *refs[-3:]),
        grid=(count,),
        in_specs=[elsewhere] * len(idle)
        + [whole(forward.shape), whole(back.shape), whole(weights.shape)]
        + [in_spec] * len(pieces),
        out_specs=out_specs + [elsewhere] * len(held),
        out_shape=out_shape + [hbm(*array.shape) for array in held],
        input_output_aliases=aliases,
        scratch_shapes=[
            pltpu.VMEM((2 * channels * mode_count, lanes), jnp.float32),
            pltpu.VMEM((2 * channels * mode_count, lanes), jnp.float32),
            pltpu.VMEM((total * channels, lanes), jnp.float32),
        ],
        compiler_params=pltpu.CompilerParams(vmem_limit_bytes=VMEM_BYTES),
        cost_estimate=cost(kernel_name, 0),
        name="line_branch",
    )(*in_hbm(idle), forward, back, *in_hbm([weights, *pieces]))


def last_kernel(ft_ref, it_ref, mix_ref, x_ref, out_ref, spectra, mixed, wide):
    channels, rows, cols, length = x_ref.shape
    mode_count = mix_ref.shape[0]
    cells = rows * cols

    def forward(pair, _):
        channel = 2 * pair
        right = jnp.concatenate(
            [x_ref[channel + at].reshape(cells, length) for at in range(2)], axis=0
        )
        keep_spectra(
            spectra, mm(ft_ref[...], right, (1, 1)), channel, mode_count, channels, cells
        )
        return 0

    lax.fori_loop(0, channels // 2, forward, 0, unroll=4)
    mix_modes(mix_ref, spectra, mixed)

    def inverse(pair, _):
        channel = 2 * pair
        result = mm(mixed_pair(mixed, channel, 2 * mode_count), it_ref[...], (0, 0))
        for at in range(2):
            wide[pl.ds(channel + at, cells, stride=channels), :] = result[
                at * cells : (at + 1) * cells
            ]
        return 0

    lax.fori_loop(0, channels // 2, inverse, 0, unroll=4)
    out_ref[...] = wide[...].reshape(rows, cols, channels, length).astype(jnp.bfloat16)


def last_branch(kernel_name, field, weights, part, parts, done, after, held=()):
    channels, rows, cols, length = field.shape
    mode_count = weights.shape[0]
    block = max(1, min(rows // parts, 128 // cols))
    steps = rows // block // parts
    forward, back = forward_rows(length, mode_count), inverse_rows(length, mode_count)
    whole = lambda shape: pl.BlockSpec(shape, lambda g: (0,) * len(shape))
    elsewhere = pl.BlockSpec(memory_space=pl.ANY)
    kept = ([] if done is None else [done]) + list(held)
    moved = 1 if done is None else 0
    idle = kept + list(after)
    return pl.pallas_call(
        lambda *refs: last_kernel(*refs[len(idle) : len(idle) + 5], *refs[-3:]),
        grid=(steps,),
        in_specs=[elsewhere] * len(idle)
        + [
            whole(forward.shape),
            whole(back.shape),
            whole(weights.shape),
            pl.BlockSpec(
                (channels, block, cols, length), lambda g: (0, part * steps + g, 0, 0)
            ),
        ],
        out_specs=[
            pl.BlockSpec((block, cols, channels, length), lambda g: (part * steps + g, 0, 0, 0))
        ]
        + [elsewhere] * len(held),
        out_shape=[hbm(rows, cols, channels, length)] + [hbm(*array.shape) for array in held],
        input_output_aliases={at: moved + at for at in range(len(kept))},
        scratch_shapes=[
            pltpu.VMEM((2 * channels * mode_count, block * cols), jnp.float32),
            pltpu.VMEM((2 * channels * mode_count, block * cols), jnp.float32),
            pltpu.VMEM((block * cols * channels, length), jnp.float32),
        ],
        compiler_params=pltpu.CompilerParams(vmem_limit_bytes=VMEM_BYTES),
        cost_estimate=cost(kernel_name, 0),
        name="last_branch",
    )(*in_hbm(idle), forward, back, *in_hbm([weights, field]))


def cell_kernel(col_ways, me_ref, x_ref, win_ref, wout_ref, bin_ref, bout_ref, *refs):
    first_ref, second, third_ref = refs[0], refs[1 : 1 + col_ways], refs[1 + col_ways]
    out_ref, now, wide = refs[-3:]
    channels, rows, ways, lanes = x_ref.shape

    for step in range(col_ways):

        @pl.when(pl.program_id(0) == step)
        def _():
            now[...] = second[step][...]

    for row in range(rows):
        for col in range(0, ways, 2):
            summed = []
            for place in (col, col + 1):
                pair = first_ref[place, row].astype(jnp.float32)
                pair = (pair + now[row, place].astype(jnp.float32)).astype(jnp.bfloat16)
                total = pair.astype(jnp.float32) + third_ref[row, place].astype(jnp.float32)
                summed.append(total.astype(jnp.bfloat16))
            scaled = mm(win_ref[...], jnp.concatenate(summed, axis=1)) * HALF_ROOT + bin_ref[...]
            hidden = (scaled + scaled * lax.erf(scaled)).astype(jnp.bfloat16)
            result = mm(wout_ref[...], hidden) * HALF_ROOT + bout_ref[...]
            for at in range(2):
                wide[row, pl.ds(col + at, channels, stride=ways), :] = result[
                    :, at * lanes : (at + 1) * lanes
                ]
        total = wide[row].reshape(channels, ways, lanes) + x_ref[:, row].astype(jnp.float32)
        out_ref[:, row] = total.astype(jnp.bfloat16)


def cells(kernel_name, field, first, base, second, third, ffn, chunk, begin, count, me, done, after):
    channels, rows, cols, lanes = field.shape
    ways, col_ways = first.shape[0], len(second)
    across = rows // col_ways
    block = 2 if begin % 2 == 0 and count % 2 == 0 else 1
    first = first.reshape(ways, -1, col_ways, channels, lanes)
    base, begin, steps = base // (col_ways * block), begin // block, count // block

    def row(step, at, me):
        return (me[1] ^ step) * (across // block) + begin + at

    def own_row(which):
        def index(step, at, me):
            now = jnp.where(step == which, at, jnp.where(step < which, 0, steps - 1))
            return begin + now, chunk, 0, 0

        return pl.BlockSpec((block, ways, channels, lanes), index)

    whole = lambda shape: pl.BlockSpec(shape, lambda *_: (0,) * len(shape))
    tile = pl.BlockSpec(
        (channels, block, ways, lanes), lambda s, a, me: (0, row(s, a, me), chunk, 0)
    )
    in_specs = [tile] + [whole(w.shape) for w in ffn]
    in_specs.append(
        pl.BlockSpec(
            (ways, block, None, channels, lanes),
            lambda s, a, me: (0, base + a, me[1] ^ s, 0, 0),
        )
    )
    in_specs += [own_row(step) for step in range(col_ways)]
    in_specs.append(
        pl.BlockSpec((block, ways, channels, lanes), lambda s, a, me: (row(s, a, me), chunk, 0, 0))
    )
    operands = [me, *in_hbm([field]), *ffn, *in_hbm([first, *second, third])]
    aliases = {}
    if done is not None:
        aliases = {len(operands): 0}
    for array in (done, after):
        if array is not None:
            in_specs.append(pl.BlockSpec(memory_space=pl.ANY))
            operands += in_hbm([array])
    return pl.pallas_call(
        functools.partial(cell_kernel, col_ways),
        grid_spec=pltpu.PrefetchScalarGridSpec(
            num_scalar_prefetch=1,
            grid=(col_ways, steps),
            in_specs=in_specs,
            out_specs=tile,
            scratch_shapes=[
                pltpu.VMEM((block, ways, channels, lanes), jnp.bfloat16),
                pltpu.VMEM((block, channels * ways, lanes), jnp.float32),
            ],
        ),
        out_shape=hbm(*field.shape),
        input_output_aliases=aliases,
        compiler_params=pltpu.CompilerParams(vmem_limit_bytes=VMEM_BYTES),
        cost_estimate=cost(kernel_name, 0),
        name="feed_forward",
    )(*operands)


def swap(piece, axis, step):
    ways = lax.axis_size(axis)
    return lax.ppermute(piece, axis, [(at, at ^ step) for at in range(ways)])


def exchange(pieces, axis):
    return [swap(piece, axis, step) if step else piece for step, piece in enumerate(pieces)]


def trade(stack):
    return lax.all_to_all(stack, "row", split_axis=0, concat_axis=0)


def body(field, spec_first, spec_second, spec_third, ffn_in, ffn_out, bias_in, bias_out):
    channels, rows, cols, lanes = field.shape
    ways, col_ways = lax.axis_size("row"), lax.axis_size("col")
    row_me, col_me = lax.axis_index("row"), lax.axis_index("col")
    me = jnp.stack([row_me, col_me]).astype(jnp.int32)
    chunks = cols // ways
    across = rows // col_ways
    ffn = (ffn_in.T, ffn_out.T, bias_in[:, None] * HALF_ROOT, bias_out[:, None])

    early_count = max(1, chunks // 2)
    rest = chunks - early_count
    early = pack("pack0", field, 0, early_count, ways, [])
    early_in = trade(early)
    side = rows_first(field, col_ways, me, early)
    side_in = exchange(side, "col")
    first_mix, second_mix, third_mix = mix_rows(side[0], spec_first, spec_second, spec_third)
    (third,) = last_branch("last0", field, third_mix, 0, 2, None, [])
    (third,) = last_branch("last1", field, third_mix, 1, 2, third, [])
    late_in = trade(pack("pack1", field, early_count, rest, ways, [third]))
    (parts,) = along_lines(
        "dim1",
        early_in,
        first_mix,
        0,
        early_count,
        [third],
        groups=col_ways,
        outs=[(early_count * rows, rows, 0)],
    )
    cut = across // 2
    second = along_lines("dim2a", side_in, second_mix, 0, cut, [parts], me=col_me)
    *second, parts = along_lines(
        "dim2b", side_in, second_mix, cut, across - cut, [], me=col_me, done=second, held=[parts]
    )
    second_in = exchange(second, "col")
    after = [second[0], *second_in[1:]]
    small = max(1, across // 4)
    if rest == 2:
        (middle,) = along_lines(
            "late0",
            late_in,
            first_mix,
            0,
            1,
            after,
            groups=col_ways,
            outs=[(rows, rows, 0)],
        )
        sizes = [col_ways * (across - small), col_ways * small]
        most, end, middle = along_lines(
            "late1",
            late_in,
            first_mix,
            1,
            1,
            [],
            groups=col_ways,
            outs=[(size, size, 0) for size in sizes],
            held=[middle],
        )
        back = [parts, middle, most, end]
    else:
        (late,) = along_lines(
            "late0", late_in, first_mix, 0, rest, after, groups=col_ways, outs=[(rest * rows, rows, 0)]
        )
        back = [parts, late]
    back = [trade(array) for array in back]

    calls = [(0, chunk * rows, chunk, 0, across) for chunk in range(early_count)]
    if rest == 2:
        calls.append((1, 0, early_count, 0, across))
        calls.append((2, 0, early_count + 1, 0, across - small))
        calls.append((3, 0, early_count + 1, across - small, small))
    else:
        calls += [(1, at * rows, early_count + at, 0, across) for at in range(rest)]
    result, token = None, late_in if rest != 2 else end
    for at, (array, base, chunk, begin, count) in enumerate(calls):
        result = cells(
            f"ffn{at}",
            field,
            back[array],
            base,
            second_in,
            third,
            ffn,
            chunk,
            begin,
            count,
            me,
            result,
            token,
        )
        token = None
    return result


def solution(mesh):
    return jax.shard_map(
        body,
        mesh=mesh,
        in_specs=(P("grp", "row", "col", None), P(), P(), P(), P(), P(), P(), P()),
        out_specs=P("grp", "row", "col", None),
        check_vma=False,
    )
```
